256 devices in a mesh: aux: 4 (over y), blk: 64 (over z, x, core).
Axes of the slice: x: 4, y: 4, z: 8, core: 2. Of those that a mesh axis runs over, the one named last changes fastest.
Arguments:
- integrals: bfloat16 [2048, 64, 8192], P(('aux', 'blk')), may hold values from -0.5 to 0.5
- metric: bfloat16 [2048, 512], P('aux'), may hold values from -1 to 2
- pair_list: int32 [127, 2], replicated, may hold values from 0 to 63, as said below
- aux_mask: int32 [16, 64], P('aux'), may hold values 0 or 1
Outputs:
- band_rows: float32 [64, 128, 640], P('blk', 'aux')
The draws below stay inside these ranges and needn't reach their ends.
Inputs may be any that keep to these rules, and one draw needn't show every extreme that they name: `pair_list`: every pair (r, r) appears once; the other rows are distinct pairs (r, r + 1) or (r, r + 2) with both blocks below 64; 63 such rows.
All inputs are finite; a program needn't handle non-finite values. No bound on the sum of `aux_mask` on one device may be relied on, other than what follows from the above.
Results may differ from the reference program's by a relative error of at most 0.0015.
Values may be sent and summed in bfloat16 or wider, within the bound.
No kernel may reach another device: no remote copies, remote signals or barrier semaphores. Data moves between devices by JAX's collectives and lax.ppermute only.
A program may use at most 128 MiB of HBM per device.

```python
import math
import jax
import jax.numpy as jnp
from jax import lax

NOCC = 64
QSH = 512
BS = 128
QB = 128
SPAN = 3
NAUX = 2048
NBLK = 64
NQB = 16
N_AUX = 4


def draw_metric(key, part):
    noise_part = jax.random.normal(key, (NAUX, QSH), jnp.float32)
    noise_part = jnp.clip(noise_part, -4.0, 4.0) * (0.5 / math.sqrt(QSH))
    identity = jnp.tile(jnp.eye(QSH, dtype=jnp.float32), (NAUX // QSH, 1))
    return (identity + noise_part).astype(jnp.bfloat16)


def draw_pair_list(key, part):
    first_ids = jnp.arange(NBLK - 1, dtype=jnp.int32)
    second_ids = jnp.arange(NBLK - 2, dtype=jnp.int32)
    rows_off = jnp.concatenate([first_ids, second_ids])
    cols_off = jnp.concatenate([first_ids + 1, second_ids + 2])
    chosen = jax.random.permutation(jax.random.fold_in(key, 11), 2 * NBLK - 3)[:NBLK - 1]
    diagonal = jnp.arange(NBLK, dtype=jnp.int32)
    row_ids = jnp.concatenate([diagonal, rows_off[chosen]])
    col_ids = jnp.concatenate([diagonal, cols_off[chosen]])
    return jnp.stack([row_ids, col_ids], axis=1).astype(jnp.int32)


def plant(drawn, key, low, high):
    longest = drawn.shape.index(max(drawn.shape))
    spots = []
    for shift in (0, 1):
        where = [jax.random.randint(jax.random.fold_in(key, axis), (), 0, length) for axis, length in enumerate(drawn.shape)]
        where[longest] = (where[longest] + shift) % drawn.shape[longest]
        spots.append(tuple(where))
    return drawn.at[spots[0]].set(low).at[spots[1]].set(high)


def steps_of(rng, extent, cuts, low, top_value):
    def one(dim, blocks):
        steps = jax.random.uniform(jax.random.fold_in(jax.random.fold_in(rng, 6), dim), (blocks,), jnp.float32, low / len(cuts), top_value / len(cuts))
        return jnp.repeat(jnp.exp(steps), extent[dim] // blocks).reshape((-1,) + (1,) * (len(extent) - dim - 1))

    loudness = one(*cuts[0])
    for cut in cuts[1:]:
        loudness = loudness * one(*cut)
    return loudness


def normal_values(own_key, extent, spread, bound, cuts=(), kind=jnp.bfloat16):
    array = jax.random.normal(own_key, extent, jnp.float32) * spread
    if len(cuts) > 0:
        array = steps_of(own_key, extent, cuts, -0.22, 0.18) * array
    return jnp.clip(array, min=-bound, max=bound).astype(kind)


def setup_inputs(seed: int = 0) -> dict:
    keys = jax.random.split(jax.random.key(seed), 5)
    integrals = normal_values(keys[0], (NAUX, NOCC, NBLK * BS), 0.07, 0.5, ((0, 256),))
    metric = draw_metric(jax.random.fold_in(keys[4], 71), 0)
    pair_list = draw_pair_list(jax.random.fold_in(keys[4], 71), 0)
    aux_mask = plant((jax.random.randint(keys[3], (NQB, NBLK), 0, 4) < 3).astype(jnp.int32), jax.random.fold_in(keys[3], 1), 0, 1)
    return {"integrals": integrals, "metric": metric, "pair_list": pair_list, "aux_mask": aux_mask}


def fit_all(integrals, metric, aux_mask):
    domains = metric.reshape(N_AUX, QSH, QSH).astype(jnp.float32)
    row_masks = jnp.repeat(aux_mask, QB, axis=0).astype(jnp.float32)

    def fit_one(block_id):
        columns = lax.dynamic_slice_in_dim(integrals, block_id * BS, BS, 2).astype(jnp.float32)
        columns = columns.reshape(N_AUX, QSH, NOCC, BS)
        fitted = jnp.einsum("apq,aqin->apin", domains, columns).reshape(NAUX, NOCC, BS)
        keep_rows = lax.dynamic_slice_in_dim(row_masks, block_id, 1, 1)
        return (fitted * keep_rows[:, :, None]).astype(jnp.bfloat16)

    return lax.map(fit_one, jnp.arange(NBLK, dtype=jnp.int32))


def reference(integrals, metric, pair_list, aux_mask):
    fitted = fit_all(integrals, metric, aux_mask)
    block_ids = jnp.arange(NBLK, dtype=jnp.int32)
    offsets = jnp.arange(SPAN, dtype=jnp.int32)
    col_gap = pair_list[:, 1] - pair_list[:, 0]
    hits = (pair_list[:, 0][:, None, None] == block_ids[None, :, None]) & (col_gap[:, None, None] == offsets[None, None, :])
    listed = jnp.sum(hits.astype(jnp.int32), axis=0).astype(jnp.float32)

    def row_tiles(block_id):
        own_block = fitted[block_id].reshape(-1, BS).astype(jnp.float32)
        tile_list = []
        for distance in range(SPAN):
            partner_id = jnp.minimum(block_id + distance, NBLK - 1)
            partner = fitted[partner_id].reshape(-1, BS).astype(jnp.float32)
            tile_list.append(lax.dot_general(own_block, partner, (((0,), (0,)), ((), ())), preferred_element_type=jnp.float32))
        return jnp.stack(tile_list)

    upper_tiles = lax.map(row_tiles, block_ids) * listed[:, :, None, None]
    pieces = []
    for column_slot in range(2 * SPAN - 1):
        offset = column_slot - (SPAN - 1)
        if offset >= 0:
            pieces.append(upper_tiles[:, offset])
        else:
            distance = -offset
            shifted = jnp.concatenate([jnp.zeros((distance, BS, BS), jnp.float32), upper_tiles[: NBLK - distance, distance]], axis=0)
            pieces.append(jnp.swapaxes(shifted, 1, 2))
    return jnp.concatenate(pieces, axis=2)
```

```python
import jax
import jax.numpy as jnp
from jax import lax
from jax.experimental import pallas as pl
from jax.experimental.pallas import tpu as pltpu
from jax.sharding import PartitionSpec as P

BS = 128
QB = 128
NZ = 8
NC = 8
NY = 4
PAIR = 2 * BS
BAND = 5
ORDER = (0, 3, 1, 2)
VMEM = pltpu.MemorySpace.VMEM
SMEM = pltpu.MemorySpace.SMEM


def fit_kernel(rows_ref, perm_ref, metric_ref, mask_ref, out_ref, turned_ref):
    groups = rows_ref.shape[0] // 256
    per = 256 // 8

    def turn(g, carry):
        start = pl.multiple_of(g * 256, 256)
        turned = jnp.dot(perm_ref[...], rows_ref[pl.ds(start, 256), :], preferred_element_type=jnp.float32)
        turned = turned.astype(jnp.bfloat16)
        at = pl.multiple_of(g * per, per)
        for i in range(8):
            turned_ref[i, pl.ds(at, per), :] = turned[i * per : (i + 1) * per]
        return carry

    lax.fori_loop(0, groups, turn, 0, unroll=2)
    width = rows_ref.shape[1]

    def fit(i, carry):
        fitted = jnp.dot(metric_ref[...], turned_ref[i], preferred_element_type=jnp.float32)
        for q in range(4):
            for b in range(width // BS):
                piece = fitted[q * QB : (q + 1) * QB, b * BS : (b + 1) * BS] * mask_ref[q, b]
                out_ref[i, q * QB : (q + 1) * QB, b * BS : (b + 1) * BS] = piece.astype(jnp.bfloat16)
        return carry

    lax.fori_loop(0, 8, fit, 0)


def fit_chunk(rows, perm, metric, mask):
    width = rows.shape[1]
    return pl.pallas_call(
        fit_kernel,
        out_shape=jax.ShapeDtypeStruct((8, 512, width), jnp.bfloat16),
        in_specs=[pl.BlockSpec(memory_space=VMEM)] * 3 + [pl.BlockSpec(memory_space=SMEM)],
        out_specs=pl.BlockSpec(memory_space=VMEM),
        scratch_shapes=[pltpu.VMEM((8, 512, width), jnp.bfloat16)],
        compiler_params=pltpu.CompilerParams(vmem_limit_bytes=24 << 20),
        cost_estimate=pl.CostEstimate(flops=2 * 4096 * width * 768, bytes_accessed=4 * 4096 * width, transcendentals=0),
        name="fit_chunk",
    )(rows, perm, metric, mask)


def band_kernel(f0, f1, f2, f3, below, above, out_ref):
    pairs = [below, f0, f1, f2, f3, above]
    for u in range(4):
        left = pairs[u + 1][...].T
        for v in (u - 1, u, u + 1):
            part = jnp.dot(left, pairs[v + 1][...], preferred_element_type=jnp.float32)
            for s in range(2):
                for t in range(2):
                    e = 2 * v + t - 2 * u - s
                    if abs(e) > 2:
                        continue
                    tile = part[s * BS : (s + 1) * BS, t * BS : (t + 1) * BS]
                    for a in range(NY):
                        out_ref[a, 2 * u + s, :, (e + 2) * BS : (e + 3) * BS] = tile[a * 32 : (a + 1) * 32]


def band_partials(pairs, below, above):
    args = [f.reshape(4096, PAIR) for f in (*pairs, below, above)]
    return pl.pallas_call(
        band_kernel,
        out_shape=jax.ShapeDtypeStruct((NY, NC, 32, BAND * BS), jnp.float32),
        in_specs=[pl.BlockSpec(memory_space=VMEM)] * 6,
        out_specs=pl.BlockSpec(memory_space=VMEM),
        compiler_params=pltpu.CompilerParams(vmem_limit_bytes=40 << 20),
        cost_estimate=pl.CostEstimate(flops=2 * 4096 * 256 * 256 * 12, bytes_accessed=16 << 20, transcendentals=0),
        name="band_partials",
    )(*args)


def local(integrals, metric, pair_list, aux_mask):
    blk = lax.axis_index("blk")
    y = lax.axis_index("aux")
    z, c = blk // NC, blk % NC
    up = [(k, k + 1) for k in range(NZ * NC) if k % NC < NC - 1]
    down = [(b, a) for a, b in up]

    row = lax.broadcasted_iota(jnp.int32, (256, 256), 0)
    col = lax.broadcasted_iota(jnp.int32, (256, 256), 1)
    perm = ((row // 32 == col % 8) & (row % 32 == col // 8)).astype(jnp.bfloat16)
    own_mask = lax.dynamic_slice(aux_mask, (0, c * 8), (4, 8)).astype(jnp.float32)

    e = jnp.arange(BAND, dtype=jnp.int32) - 2
    low, high = blk + jnp.minimum(e, 0), blk + jnp.maximum(e, 0)
    hits = (pair_list[:, 0][:, None] == low[None]) & (pair_list[:, 1][:, None] == high[None])
    scale = jnp.repeat(jnp.sum(hits.astype(jnp.float32), axis=0), BS)

    split = integrals.reshape(8, NZ, 8, NC, 4, PAIR)
    pairs = [None] * 4
    below = above = None
    for u in ORDER:
        send = split[:, :, :, :, u].transpose(1, 3, 0, 2, 4).reshape(NZ * NC, 64, PAIR)
        got = lax.all_to_all(send, "blk", split_axis=0, concat_axis=0, tiled=True)
        pairs[u] = fit_chunk(got.reshape(4096, PAIR), perm, metric, own_mask[:, 2 * u : 2 * u + 2])
        if u == 0:
            above = lax.ppermute(pairs[u], "blk", down)
        if u == 3:
            below = lax.ppermute(pairs[u], "blk", up)
    parts = band_partials(pairs, below, above)

    total = lax.dynamic_index_in_dim(parts, y, 0, keepdims=False)
    for d in range(1, NY):
        piece = lax.dynamic_index_in_dim(parts, (y + d) % NY, 0, keepdims=False)
        total = total + lax.ppermute(piece, "aux", [(a, (a + d) % NY) for a in range(NY)])

    rows = None
    for t in range(NZ):
        piece = lax.dynamic_index_in_dim(total, (z + t) % NC, 0, keepdims=False)
        moves = [(zz * NC + cc, cc * NC + (zz + t) % NC) for zz in range(NZ) for cc in range(NC)]
        got = lax.ppermute(piece, "blk", moves)
        rows = got if rows is None else rows + got
    return (rows * scale[None, :])[None]


def solution(mesh):
    return jax.shard_map(
        local,
        mesh=mesh,
        in_specs=(P(("aux", "blk"), None, None), P("aux", None), P(), P("aux", None)),
        out_specs=P("blk", "aux", None),
        check_vma=False,
    )
```

```python
import jax
import jax.numpy as jnp
from jax import lax
from jax.experimental import pallas as pl
from jax.experimental.pallas import tpu as pltpu
from jax.sharding import PartitionSpec as P

BS = 128
QB = 128
NZ = 8
NC = 8
NY = 4
PAIR = 2 * BS
BAND = 5
PART = BS // NY
VMEM = pltpu.MemorySpace.VMEM
SMEM = pltpu.MemorySpace.SMEM


def in_band(u, v):
    found = []
    for s in range(2):
        for t in range(2):
            e = 2 * v + t - 2 * u - s
            if abs(e) <= 2 and 0 <= u <= 3:
                found.append((s, t, 2 * u + s, e))
    return found


EARLY_PRODUCTS = ((0, -1), (0, 0), (0, 1), (1, 1), (3, 3), (3, 4))
LATE_PRODUCTS = ((2, 1), (2, 2), (2, 3))


def slots_of(products):
    slots = []
    for u, v in products:
        slots += [(r, e) for _, _, r, e in in_band(u, v)]
        if u != v:
            slots += [(r, e) for _, _, r, e in in_band(v, u)]
    off = [k for k in slots if k[1] != 0]
    return off + [k for k in slots if k[1] == 0], len(off)


EARLY, EARLY_OFF = slots_of(EARLY_PRODUCTS)
LATE, LATE_OFF = slots_of(LATE_PRODUCTS)


def sent_slots(slots, off):
    return 2 * len(slots) - off


def cut_kernel(source, out_ref, sem, *, offsets):
    def one(k, carry):
        z, c = k // NC, k % NC
        for n, offset in enumerate(offsets):
            start = pl.multiple_of(c * 1024 + offset, BS)
            pltpu.make_async_copy(
                source.at[:, z, :, pl.ds(start, PAIR)], out_ref.at[k, :, :, pl.ds(n * PAIR, PAIR)], sem
            ).start()
        return carry

    lax.fori_loop(0, NZ * NC, one, 0)
    pltpu.make_async_copy(out_ref, out_ref, sem).wait()


def cut_chunk(integrals, pairs):
    width = PAIR * len(pairs)
    return pl.pallas_call(
        lambda s, o, sem: cut_kernel(s, o, sem, offsets=[PAIR * u for u in pairs]),
        out_shape=jax.ShapeDtypeStruct((NZ * NC, 8, 8, width), jnp.bfloat16),
        in_specs=[pl.BlockSpec(memory_space=pl.ANY)],
        out_specs=pl.BlockSpec(memory_space=VMEM),
        scratch_shapes=[pltpu.SemaphoreType.DMA],
        compiler_params=pltpu.CompilerParams(vmem_limit_bytes=60 << 20),
        cost_estimate=pl.CostEstimate(flops=0, bytes_accessed=2 * 8192 * width, transcendentals=0),
        name="cut_chunk",
    )(integrals.reshape(8, NZ, 8, NC * 1024))


def turn_rows(rows_ref, perm_ref, turned_ref):
    def turn(g, carry):
        start = pl.multiple_of(g * 256, 256)
        turned = jnp.dot(perm_ref[...], rows_ref[pl.ds(start, 256), :], preferred_element_type=jnp.float32)
        turned = turned.astype(jnp.bfloat16)
        at = pl.multiple_of(g * 32, 32)
        for i in range(8):
            turned_ref[i, pl.ds(at, 32), :] = turned[i * 32 : (i + 1) * 32]
        return carry

    lax.fori_loop(0, 16, turn, 0, unroll=4)


def fit_one(metric_ref, turned_ref, mask_ref, fitted_ref, i):
    fitted = jnp.dot(metric_ref[...], turned_ref[i], preferred_element_type=jnp.float32)
    for q in range(4):
        for b in range(2):
            piece = fitted[q * QB : (q + 1) * QB, b * BS : (b + 1) * BS] * mask_ref[q, b]
            at = pl.multiple_of(i * 512, 512) + q * QB
            fitted_ref[pl.ds(at, QB), b * BS : (b + 1) * BS] = piece.astype(jnp.bfloat16)


def fit_kernel(rows_ref, perm_ref, metric_ref, mask_ref, out_ref, turned_ref):
    turn_rows(rows_ref, perm_ref, turned_ref)

    def fit(i, carry):
        fit_one(metric_ref, turned_ref, mask_ref, out_ref, i)
        return carry

    lax.fori_loop(0, 8, fit, 0, unroll=2)


def whole(shape, at=None):
    return pl.BlockSpec(shape, lambda g: at or (0,) * len(shape))


def fit_chunk(rows, at, perm, metric, mask):
    return pl.pallas_call(
        fit_kernel,
        grid=(1,),
        out_shape=jax.ShapeDtypeStruct((4096, PAIR), jnp.bfloat16),
        in_specs=[
            whole((4096, PAIR), (0, at)),
            whole((256, 256)),
            whole((512, 512)),
            pl.BlockSpec(memory_space=SMEM),
        ],
        out_specs=whole((4096, PAIR)),
        scratch_shapes=[pltpu.VMEM((8, 512, PAIR), jnp.bfloat16)],
        compiler_params=pltpu.CompilerParams(vmem_limit_bytes=24 << 20),
        cost_estimate=pl.CostEstimate(flops=2 * 4096 * PAIR * 768, bytes_accessed=4 * 4096 * PAIR, transcendentals=0),
        name="fit_chunk",
    )(rows, perm, metric, mask)


def put_slots(tile_ref, places, slots, off, y, own_ref, out_refs):
    for s, t, r, e in places:
        n = slots.index((r, e))
        for d in range(NY):
            at = pl.multiple_of(s * BS + lax.rem(y + d, NY) * PART, PART)
            piece = tile_ref[pl.ds(at, PART), t * BS : (t + 1) * BS]
            if d == 0:
                own_ref[n] = piece
                continue
            high = piece.astype(jnp.bfloat16)
            out_refs[d - 1][n] = high
            if e == 0:
                out_refs[d - 1][n + len(slots) - off] = (piece - high.astype(jnp.float32)).astype(jnp.bfloat16)


def put_product(u, v, tile_ref, flip_ref, slots, off, y, own_ref, out_refs):
    put_slots(tile_ref, in_band(u, v), slots, off, y, own_ref, out_refs)
    if u != v and 0 <= v <= 3:
        flip_ref[...] = tile_ref[...].T
        put_slots(flip_ref, in_band(v, u), slots, off, y, own_ref, out_refs)


def early_kernel(y_ref, f0, f1, f3, below, above, own_ref, o1, o2, o3, tiles_ref, flips_ref):
    pairs = {-1: below, 0: f0, 1: f1, 3: f3, 4: above}
    lefts = {}
    for n, (u, v) in enumerate(EARLY_PRODUCTS):
        if u not in lefts:
            lefts = {u: pairs[u][...].T}
        tiles_ref[n] = jnp.dot(lefts[u], pairs[v][...], preferred_element_type=jnp.float32)
        put_product(u, v, tiles_ref.at[n], flips_ref.at[n], EARLY, EARLY_OFF, y_ref[0], own_ref, (o1, o2, o3))


def late_kernel(y_ref, mask_ref, rows_ref, perm_ref, metric_ref, f1, f3, own_ref, o1, o2, o3, turned_ref, f2, tiles_ref, flips_ref):
    turn_rows(rows_ref, perm_ref, turned_ref)
    tiles_ref[...] = jnp.zeros_like(tiles_ref)

    def step(i, carry):
        fit_one(metric_ref, turned_ref, mask_ref, f2, i)
        at = pl.multiple_of(i * 512, 512)
        left = f2[pl.ds(at, 512), :].T
        for n, right in enumerate((f1, f2, f3)):
            tiles_ref[n] += jnp.dot(left, right[pl.ds(at, 512), :], preferred_element_type=jnp.float32)
        return carry

    lax.fori_loop(0, 8, step, 0)
    for n, (u, v) in enumerate(LATE_PRODUCTS):
        put_product(u, v, tiles_ref.at[n], flips_ref.at[n], LATE, LATE_OFF, y_ref[0], own_ref, (o1, o2, o3))


def exchange_shapes(slots, off):
    sent = jax.ShapeDtypeStruct((sent_slots(slots, off), PART, BS), jnp.bfloat16)
    return [jax.ShapeDtypeStruct((len(slots), PART, BS), jnp.float32)] + [sent] * 3


def early_tiles(y, f0, f1, f3, below, above):
    count = len(EARLY_PRODUCTS)
    return pl.pallas_call(
        early_kernel,
        out_shape=exchange_shapes(EARLY, EARLY_OFF),
        in_specs=[pl.BlockSpec(memory_space=SMEM)] + [pl.BlockSpec(memory_space=VMEM)] * 5,
        out_specs=[pl.BlockSpec(memory_space=VMEM)] * 4,
        scratch_shapes=[pltpu.VMEM((count, PAIR, PAIR), jnp.float32)] * 2,
        compiler_params=pltpu.CompilerParams(vmem_limit_bytes=40 << 20),
        cost_estimate=pl.CostEstimate(flops=2 * 4096 * 256 * 256 * count, bytes_accessed=14 << 20, transcendentals=0),
        name="early_tiles",
    )(y, f0, f1, f3, below, above)


def late_tiles(y, mask, rows, perm, metric, f1, f3):
    return pl.pallas_call(
        late_kernel,
        out_shape=exchange_shapes(LATE, LATE_OFF),
        in_specs=[pl.BlockSpec(memory_space=SMEM)] * 2 + [pl.BlockSpec(memory_space=VMEM)] * 5,
        out_specs=[pl.BlockSpec(memory_space=VMEM)] * 4,
        scratch_shapes=[
            pltpu.VMEM((8, 512, PAIR), jnp.bfloat16),
            pltpu.VMEM((4096, PAIR), jnp.bfloat16),
            pltpu.VMEM((3, PAIR, PAIR), jnp.float32),
            pltpu.VMEM((3, PAIR, PAIR), jnp.float32),
        ],
        compiler_params=pltpu.CompilerParams(vmem_limit_bytes=40 << 20),
        cost_estimate=pl.CostEstimate(flops=2 * 4096 * 256 * 1536, bytes_accessed=8 << 20, transcendentals=0),
        name="late_tiles",
    )(y, mask, rows, perm, metric, f1, f3)


def over_domains(sent):
    return [lax.ppermute(s, "aux", [(a, (a + d) % NY) for a in range(NY)]) for d, s in enumerate(sent, 1)]


def widen(got, slots, off):
    high = got[: len(slots)].astype(jnp.float32)
    low = got[len(slots) :].astype(jnp.float32)
    return high + jnp.pad(low, ((off, 0), (0, 0), (0, 0)))


def merge_kernel(odd_ref, early_ref, late_ref, g1, g2, g3, own_ref, out_ref, band_ref):
    for n, (r, e) in enumerate(EARLY):
        band_ref[r, e + 2] = early_ref[n]
    for n, (r, e) in enumerate(LATE):
        value = late_ref[n]
        for got in (g1, g2, g3):
            value = value + got[n].astype(jnp.float32)
            if e == 0:
                value = value + got[n + len(LATE) - LATE_OFF].astype(jnp.float32)
        band_ref[r, e + 2] = value
    odd = odd_ref[0]
    for k in range(4):
        for slot in range(BAND):
            own_ref[k, slot] = band_ref[2 * k + odd, slot]
            value = band_ref[2 * k + 1 - odd, slot]
            high = value.astype(jnp.bfloat16)
            out_ref[k * 6 + slot] = high
            if slot == 2:
                out_ref[k * 6 + 5] = (value - high.astype(jnp.float32)).astype(jnp.bfloat16)


def merge(odd, early, late, got):
    return pl.pallas_call(
        merge_kernel,
        out_shape=[
            jax.ShapeDtypeStruct((4, BAND, PART, BS), jnp.float32),
            jax.ShapeDtypeStruct((24, PART, BS), jnp.bfloat16),
        ],
        in_specs=[pl.BlockSpec(memory_space=SMEM)] + [pl.BlockSpec(memory_space=VMEM)] * 5,
        out_specs=[pl.BlockSpec(memory_space=VMEM)] * 2,
        scratch_shapes=[pltpu.VMEM((NC, BAND, PART, BS), jnp.float32)],
        name="merge",
    )(odd, early, late, *got)


def settle_kernel(half_ref, own_ref, got_ref, o0, o1, o2, o3):
    for j, out in enumerate((o0, o1, o2, o3)):
        k = lax.rem(half_ref[0] + j, 4)
        for slot in range(BAND):
            value = own_ref[k, slot] + got_ref[k * 6 + slot].astype(jnp.float32)
            if slot == 2:
                value = value + got_ref[k * 6 + 5].astype(jnp.float32)
            out[:, slot * BS : (slot + 1) * BS] = value


def settle(half, own, got):
    return pl.pallas_call(
        settle_kernel,
        out_shape=[jax.ShapeDtypeStruct((PART, BAND * BS), jnp.float32)] * 4,
        in_specs=[pl.BlockSpec(memory_space=SMEM)] + [pl.BlockSpec(memory_space=VMEM)] * 2,
        out_specs=[pl.BlockSpec(memory_space=VMEM)] * 4,
        name="settle",
    )(half, own, got)


def local(integrals, metric, pair_list, aux_mask):
    blk = lax.axis_index("blk")
    y = jnp.full((1,), lax.axis_index("aux"), jnp.int32)
    z, c = blk // NC, blk % NC
    grid = [(k // NC, k % NC) for k in range(NZ * NC)]
    up = [(zz * NC + cc, zz * NC + cc + 1) for zz, cc in grid if cc < NC - 1]
    down = [(b, a) for a, b in up]

    row = lax.broadcasted_iota(jnp.int32, (256, 256), 0)
    col = lax.broadcasted_iota(jnp.int32, (256, 256), 1)
    perm = ((row // 32 == col % 8) & (row % 32 == col // 8)).astype(jnp.bfloat16)
    own_mask = lax.dynamic_slice(aux_mask, (0, c * 8), (4, 8)).astype(jnp.float32)
    masks = [own_mask[:, 2 * u : 2 * u + 2] for u in range(4)]

    e = jnp.arange(BAND, dtype=jnp.int32) - 2
    low, high = blk + jnp.minimum(e, 0), blk + jnp.maximum(e, 0)
    hits = (pair_list[:, 0][:, None] == low[None]) & (pair_list[:, 1][:, None] == high[None])
    scale = jnp.repeat(jnp.sum(hits.astype(jnp.float32), axis=0), BS)

    def spread(pairs, source):
        got = lax.all_to_all(cut_chunk(source, pairs), "blk", split_axis=0, concat_axis=0, tiled=True)
        return got.reshape(4096, PAIR * len(pairs))

    rows = spread((0, 3), integrals)
    f0 = fit_chunk(rows, 0, perm, metric, masks[0])
    f3 = fit_chunk(rows, 1, perm, metric, masks[3])
    above = lax.ppermute(f0, "blk", down)
    below = lax.ppermute(f3, "blk", up)
    rows = spread((1,), integrals)
    source, above, below = lax.optimization_barrier((integrals, above, below))
    last = spread((2,), source)
    f1 = fit_chunk(rows, 0, perm, metric, masks[1])

    early, *sent = early_tiles(y, f0, f1, f3, below, above)
    for got in over_domains(sent):
        early = early + widen(got, EARLY, EARLY_OFF)

    late, *sent = late_tiles(y, masks[2], last, perm, metric, f1, f3)
    own, sent = merge(jnp.full((1,), z % 2, jnp.int32), early, late, over_domains(sent))
    got = lax.ppermute(sent, "blk", [(zz * NC + cc, (zz ^ 1) * NC + cc) for zz, cc in grid])
    total, *sent = settle(jnp.full((1,), z // 2, jnp.int32), own, got)
    for j, s in enumerate(sent, 1):
        total = total + lax.ppermute(s, "blk", [(zz * NC + cc, (zz + 2 * j) % NZ * NC + cc) for zz, cc in grid])
    total = lax.ppermute(total, "blk", [(zz * NC + cc, cc * NC + zz) for zz, cc in grid])
    return (total * scale[None, :])[None]


def solution(mesh):
    return jax.shard_map(
        local,
        mesh=mesh,
        in_specs=(P(("aux", "blk"), None, None), P("aux", None), P(), P("aux", None)),
        out_specs=P("blk", "aux", None),
        check_vma=False,
    )
```

```python
import jax
import jax.numpy as jnp
from jax import lax
from jax.experimental import pallas as pl
from jax.experimental.pallas import tpu as pltpu
from jax.sharding import PartitionSpec as P

BS = 128
QB = 128
NZ = 8
NC = 8
NY = 4
PAIR = 2 * BS
BAND = 5
PART = BS // NY
FIRST = (0, 7, 1, 2, 5, 6)
LAST = (3, 4)
VMEM = pltpu.MemorySpace.VMEM
SMEM = pltpu.MemorySpace.SMEM

EARLY_PRODUCTS = (((0, 1), (0, 1, 2)), ((6, 7), (5, 6, 7)), ((2, 5), (2, 5)))
LATE_PRODUCT = ((3, 4), (1, 2, 3, 4, 5, 6))


def tiles_of(products):
    found = {}
    for n, (rows, cols) in enumerate(products):
        for s, r in enumerate(rows):
            for t, k in enumerate(cols):
                if abs(k - r) <= 2:
                    found[r, k - r] = (n, s, t, False)
    for n, (rows, cols) in enumerate(products):
        for s, r in enumerate(rows):
            for t, k in enumerate(cols):
                if abs(k - r) <= 2 and 0 <= k < NC and (k, r - k) not in found:
                    found[k, r - k] = (n, s, t, True)
    return found


EARLY_TILES = tiles_of(EARLY_PRODUCTS)
LATE_TILES = tiles_of((LATE_PRODUCT,))
STRANGE = ((0, -2), (7, 2), (0, -1), (1, -2), (6, 2), (7, 1))


def ordered(slots):
    off = [k for k in slots if k[1] != 0]
    return off + [k for k in slots if k[1] == 0], len(off)


EARLY, EARLY_OFF = ordered(EARLY_TILES)
LATE, LATE_OFF = ordered(STRANGE + tuple(LATE_TILES))


def sent_slots(slots, off):
    return 2 * len(slots) - off


def runs(blocks):
    found = []
    for n, b in enumerate(blocks):
        if found and found[-1][0] + found[-1][2] == b * BS:
            found[-1][2] += BS
        else:
            found.append([b * BS, n * BS, BS])
    return found


def cut_kernel(source, out_ref, held, sems, *, blocks):
    half = NZ * NC // 2

    def gather(part):
        def one(n, carry):
            k = part * half + n
            z, c = k // NC, k % NC
            for start, at, width in runs(blocks):
                begin = pl.multiple_of(c * 1024 + start, BS)
                pltpu.make_async_copy(
                    source.at[:, z, :, pl.ds(begin, width)], held.at[k, :, :, pl.ds(at, width)], sems.at[part]
                ).start()
            return carry

        lax.fori_loop(0, half, one, 0)

    gather(0)
    gather(1)
    writes = []
    for part in range(2):
        here = held.at[pl.ds(part * half, half)]
        pltpu.make_async_copy(here, here, sems.at[part]).wait()
        write = pltpu.make_async_copy(here, out_ref.at[pl.ds(part * half, half)], sems.at[2 + part])
        write.start()
        writes.append(write)
    for write in writes:
        write.wait()


def cut_chunk(integrals, blocks):
    shape = (NZ * NC, 8, 8, BS * len(blocks))
    return pl.pallas_call(
        lambda *refs: cut_kernel(*refs, blocks=blocks),
        out_shape=jax.ShapeDtypeStruct(shape, jnp.bfloat16),
        in_specs=[pl.BlockSpec(memory_space=pl.ANY)],
        out_specs=pl.BlockSpec(memory_space=pl.ANY),
        scratch_shapes=[pltpu.VMEM(shape, jnp.bfloat16), pltpu.SemaphoreType.DMA((4,))],
        compiler_params=pltpu.CompilerParams(vmem_limit_bytes=60 << 20),
        cost_estimate=pl.CostEstimate(flops=0, bytes_accessed=2 * 8192 * shape[3], transcendentals=0),
        name="cut_chunk",
    )(integrals.reshape(8, NZ, 8, NC * 1024))


def turn_rows(rows_ref, perm_ref, turned_ref, first, count):
    def turn(g, carry):
        start = pl.multiple_of(g * 256, 256)
        turned = jnp.dot(perm_ref[...], rows_ref[pl.ds(start, 256), :], preferred_element_type=jnp.float32)
        turned = turned.astype(jnp.bfloat16)
        at = pl.multiple_of(g * 32, 32)
        for i in range(8):
            turned_ref[i, pl.ds(at, 32), :] = turned[i * 32 : (i + 1) * 32]
        return carry

    lax.fori_loop(first, first + count, turn, 0, unroll=4)


def fit_one(metric_ref, turned_ref, mask_ref, i):
    fitted = jnp.dot(metric_ref[...], turned_ref[i], preferred_element_type=jnp.float32)
    out = []
    for b in range(2):
        column = fitted[:, b * BS : (b + 1) * BS]
        pieces = [column[q * QB : (q + 1) * QB] * mask_ref[q, b] for q in range(4)]
        out.append(jnp.concatenate(pieces, axis=0).astype(jnp.bfloat16))
    return out


def fit_kernel(rows_ref, perm_ref, metric_ref, mask_ref, out_a, out_b, turned_ref):
    turn_rows(rows_ref, perm_ref, turned_ref, 0, 16)

    def fit(i, carry):
        at = pl.multiple_of(i * 512, 512)
        out_a[pl.ds(at, 512), :], out_b[pl.ds(at, 512), :] = fit_one(metric_ref, turned_ref, mask_ref, i)
        return carry

    lax.fori_loop(0, 8, fit, 0, unroll=2)


def whole(shape, at=None):
    return pl.BlockSpec(shape, lambda g: at or (0,) * len(shape))


def fit_chunk(rows, at, perm, metric, mask):
    return pl.pallas_call(
        fit_kernel,
        grid=(1,),
        out_shape=[jax.ShapeDtypeStruct((4096, BS), jnp.bfloat16)] * 2,
        in_specs=[
            whole((4096, PAIR), (0, at)),
            whole((256, 256)),
            whole((512, 512)),
            pl.BlockSpec(memory_space=SMEM),
        ],
        out_specs=[whole((4096, BS))] * 2,
        scratch_shapes=[pltpu.VMEM((8, 512, PAIR), jnp.bfloat16)],
        compiler_params=pltpu.CompilerParams(vmem_limit_bytes=24 << 20),
        cost_estimate=pl.CostEstimate(flops=2 * 4096 * PAIR * 768, bytes_accessed=4 * 4096 * PAIR, transcendentals=0),
        name="fit_chunk",
    )(rows, perm, metric, mask)


def put_slot(tile_ref, row, col, n, diagonal, slots, off, y, own_ref, out_refs):
    for d in range(NY):
        at = pl.multiple_of(row * BS + lax.rem(y + d, NY) * PART, PART)
        piece = tile_ref[pl.ds(at, PART), col * BS : (col + 1) * BS]
        if d == 0:
            own_ref[n] = piece
            continue
        high = piece.astype(jnp.bfloat16)
        out_refs[d - 1][n] = high
        if diagonal:
            out_refs[d - 1][n + len(slots) - off] = (piece - high.astype(jnp.float32)).astype(jnp.bfloat16)


def put_tiles(found, tiles, flip_ref, slots, off, y, own_ref, out_refs):
    flips = 0
    for r, e in slots:
        if (r, e) not in found:
            continue
        product, s, t, turned = found[r, e]
        n = slots.index((r, e))
        if not turned:
            put_slot(tiles[product], s, t, n, e == 0, slots, off, y, own_ref, out_refs)
            continue
        flip_ref[flips] = tiles[product][s * BS : (s + 1) * BS, t * BS : (t + 1) * BS].T
        put_slot(flip_ref.at[flips], 0, 0, n, False, slots, off, y, own_ref, out_refs)
        flips += 1


EARLY_BLOCKS = (0, 1, 2, 5, 6, 7)


def early_kernel(y_ref, *refs):
    blocks = dict(zip(EARLY_BLOCKS, refs[:6]))
    own_ref, o1, o2, o3, t0, t1, t2, flip_ref = refs[6:]
    tiles = (t0, t1, t2)
    for n, (rows, cols) in enumerate(EARLY_PRODUCTS):
        left = jnp.concatenate([blocks[r][...] for r in rows], axis=1).T
        right = jnp.concatenate([blocks[k][...] for k in cols], axis=1)
        tiles[n][...] = jnp.dot(left, right, preferred_element_type=jnp.float32)
    put_tiles(EARLY_TILES, tiles, flip_ref, EARLY, EARLY_OFF, y_ref[0], own_ref, (o1, o2, o3))


def edge_kernel(below, f0, f1, f6, f7, above, down_ref, up_ref, own_ref):
    low = jnp.dot(
        below[...].T, jnp.concatenate([f0[...], f1[...]], axis=1), preferred_element_type=jnp.float32
    )
    high = jnp.dot(
        above[...].T, jnp.concatenate([f6[...], f7[...]], axis=1), preferred_element_type=jnp.float32
    )
    down_ref[...] = low[:, BS:]
    up_ref[...] = high[:, :BS]
    own_ref[0] = low[:, :BS].T
    own_ref[1] = low[:, BS:].T
    own_ref[2] = high[:, :BS].T
    own_ref[3] = high[:, BS:].T


def edge_tiles(below, f0, f1, f6, f7, above):
    tile = jax.ShapeDtypeStruct((BS, BS), jnp.float32)
    return pl.pallas_call(
        edge_kernel,
        out_shape=[tile, tile, jax.ShapeDtypeStruct((4, BS, BS), jnp.float32)],
        in_specs=[pl.BlockSpec(memory_space=VMEM)] * 6,
        out_specs=[pl.BlockSpec(memory_space=VMEM)] * 3,
        compiler_params=pltpu.CompilerParams(vmem_limit_bytes=24 << 20),
        cost_estimate=pl.CostEstimate(flops=2 * 4096 * 256 * 256, bytes_accessed=6 << 20, transcendentals=0),
        name="edge_tiles",
    )(below, f0, f1, f6, f7, above)


def late_kernel(y_ref, mask_ref, rows_hbm, f1_hbm, f2_hbm, f5_hbm, f6_hbm, perm_ref, metric_ref, from_below, from_above, edges, own_ref, o1, o2, o3, rows_ref, turned_ref, left_ref, right_ref, tiles_ref, flip_ref, row_sems, sems):
    feeds = []
    for n in range(4):
        piece = pl.ds(n * 1024, 1024)
        feeds.append(pltpu.make_async_copy(rows_hbm.at[piece], rows_ref.at[piece], row_sems.at[n]))
    fits = [
        pltpu.make_async_copy(f, right_ref.at[n], sems.at[n]) for n, f in enumerate((f1_hbm, f2_hbm, f5_hbm, f6_hbm))
    ]
    for copy in feeds + fits:
        copy.start()
    for n, feed in enumerate(feeds):
        feed.wait()
        turn_rows(rows_ref, perm_ref, turned_ref, 4 * n, 4)

    def step(i, carry):
        at = pl.ds(pl.multiple_of(i * 512, 512), 512)
        left_ref[at, :BS], left_ref[at, BS:] = fit_one(metric_ref, turned_ref, mask_ref, i)
        return carry

    lax.fori_loop(0, 8, step, 0, unroll=2)
    for copy in fits:
        copy.wait()
    f1, f2, f5, f6 = [right_ref[n] for n in range(4)]
    right = jnp.concatenate([f1, f2, left_ref[...], f5, f6], axis=1)
    tiles_ref[...] = jnp.dot(left_ref[...].T, right, preferred_element_type=jnp.float32)
    y = y_ref[0]
    for tile_ref, (r, e) in zip((from_below, from_above, *(edges.at[k] for k in range(4))), STRANGE):
        put_slot(tile_ref, 0, 0, LATE.index((r, e)), False, LATE, LATE_OFF, y, own_ref, (o1, o2, o3))
    put_tiles(LATE_TILES, (tiles_ref,), flip_ref, LATE, LATE_OFF, y, own_ref, (o1, o2, o3))


def exchange_shapes(slots, off):
    sent = jax.ShapeDtypeStruct((sent_slots(slots, off), PART, BS), jnp.bfloat16)
    return [jax.ShapeDtypeStruct((len(slots), PART, BS), jnp.float32)] + [sent] * 3


def early_tiles(y, blocks):
    return pl.pallas_call(
        early_kernel,
        out_shape=exchange_shapes(EARLY, EARLY_OFF),
        in_specs=[pl.BlockSpec(memory_space=SMEM)] + [pl.BlockSpec(memory_space=VMEM)] * 6,
        out_specs=[pl.BlockSpec(memory_space=VMEM)] * 4,
        scratch_shapes=[
            pltpu.VMEM((PAIR, 3 * BS), jnp.float32),
            pltpu.VMEM((PAIR, 3 * BS), jnp.float32),
            pltpu.VMEM((PAIR, PAIR), jnp.float32),
            pltpu.VMEM((4, BS, BS), jnp.float32),
        ],
        compiler_params=pltpu.CompilerParams(vmem_limit_bytes=40 << 20),
        cost_estimate=pl.CostEstimate(flops=2 * 4096 * 256 * 1024, bytes_accessed=7 << 20, transcendentals=0),
        name="early_tiles",
    )(y, *blocks)


def late_tiles(y, mask, rows, f1, f2, f5, f6, perm, metric, from_below, from_above, edges):
    return pl.pallas_call(
        late_kernel,
        out_shape=exchange_shapes(LATE, LATE_OFF),
        in_specs=[pl.BlockSpec(memory_space=SMEM)] * 2
        + [pl.BlockSpec(memory_space=pl.ANY)] * 5
        + [pl.BlockSpec(memory_space=VMEM)] * 5,
        out_specs=[pl.BlockSpec(memory_space=VMEM)] * 4,
        scratch_shapes=[
            pltpu.VMEM((4096, PAIR), jnp.bfloat16),
            pltpu.VMEM((8, 512, PAIR), jnp.bfloat16),
            pltpu.VMEM((4096, PAIR), jnp.bfloat16),
            pltpu.VMEM((4, 4096, BS), jnp.bfloat16),
            pltpu.VMEM((PAIR, 6 * BS), jnp.float32),
            pltpu.VMEM((6, BS, BS), jnp.float32),
            pltpu.SemaphoreType.DMA((4,)),
            pltpu.SemaphoreType.DMA((4,)),
        ],
        compiler_params=pltpu.CompilerParams(vmem_limit_bytes=60 << 20),
        cost_estimate=pl.CostEstimate(flops=2 * 4096 * 256 * 1536, bytes_accessed=8 << 20, transcendentals=0),
        name="late_tiles",
    )(y, mask, rows, f1, f2, f5, f6, perm, metric, from_below, from_above, edges)


def over_domains(sent):
    return [lax.ppermute(s, "aux", [(a, (a + d) % NY) for a in range(NY)]) for d, s in enumerate(sent, 1)]


def gathered(own_ref, got_refs, n, e, slots, off):
    value = own_ref[n]
    for got in got_refs:
        value = value + got[n].astype(jnp.float32)
        if e == 0:
            value = value + got[n + len(slots) - off].astype(jnp.float32)
    return value


def early_sum_kernel(own_ref, g1, g2, g3, out_ref):
    for n, (r, e) in enumerate(EARLY):
        out_ref[n] = gathered(own_ref, (g1, g2, g3), n, e, EARLY, EARLY_OFF)


def early_sum(own, got):
    return pl.pallas_call(
        early_sum_kernel,
        out_shape=jax.ShapeDtypeStruct(own.shape, jnp.float32),
        in_specs=[pl.BlockSpec(memory_space=VMEM)] * 4,
        out_specs=pl.BlockSpec(memory_space=VMEM),
        compiler_params=pltpu.CompilerParams(vmem_limit_bytes=16 << 20),
        name="early_sum",
    )(own, *got)


def merge_kernel(odd_ref, early_ref, late_ref, g1, g2, g3, own_ref, out_ref, band_ref):
    for n, (r, e) in enumerate(EARLY):
        band_ref[r, e + 2] = early_ref[n]
    for n, (r, e) in enumerate(LATE):
        band_ref[r, e + 2] = gathered(late_ref, (g1, g2, g3), n, e, LATE, LATE_OFF)
    odd = odd_ref[0]
    for k in range(4):
        for slot in range(BAND):
            own_ref[k, slot] = band_ref[2 * k + odd, slot]
            value = band_ref[2 * k + 1 - odd, slot]
            high = value.astype(jnp.bfloat16)
            out_ref[k * 6 + slot] = high
            if slot == 2:
                out_ref[k * 6 + 5] = (value - high.astype(jnp.float32)).astype(jnp.bfloat16)


def merge(odd, early, late, got):
    return pl.pallas_call(
        merge_kernel,
        out_shape=[
            jax.ShapeDtypeStruct((4, BAND, PART, BS), jnp.float32),
            jax.ShapeDtypeStruct((24, PART, BS), jnp.bfloat16),
        ],
        in_specs=[pl.BlockSpec(memory_space=SMEM)] + [pl.BlockSpec(memory_space=VMEM)] * 5,
        out_specs=[pl.BlockSpec(memory_space=VMEM)] * 2,
        scratch_shapes=[pltpu.VMEM((NC, BAND, PART, BS), jnp.float32)],
        compiler_params=pltpu.CompilerParams(vmem_limit_bytes=16 << 20),
        name="merge",
    )(odd, early, late, *got)


def settle_kernel(half_ref, own_ref, got_ref, o0, o1, o2, o3):
    for j, out in enumerate((o0, o1, o2, o3)):
        k = lax.rem(half_ref[0] + j, 4)
        for slot in range(BAND):
            value = own_ref[k, slot] + got_ref[k * 6 + slot].astype(jnp.float32)
            if slot == 2:
                value = value + got_ref[k * 6 + 5].astype(jnp.float32)
            out[:, slot * BS : (slot + 1) * BS] = value


def settle(half, own, got):
    return pl.pallas_call(
        settle_kernel,
        out_shape=[jax.ShapeDtypeStruct((PART, BAND * BS), jnp.float32)] * 4,
        in_specs=[pl.BlockSpec(memory_space=SMEM)] + [pl.BlockSpec(memory_space=VMEM)] * 2,
        out_specs=[pl.BlockSpec(memory_space=VMEM)] * 4,
        compiler_params=pltpu.CompilerParams(vmem_limit_bytes=16 << 20),
        name="settle",
    )(half, own, got)


def local(integrals, metric, pair_list, aux_mask):
    blk = lax.axis_index("blk")
    y = jnp.full((1,), lax.axis_index("aux"), jnp.int32)
    z, c = blk // NC, blk % NC
    grid = [(k // NC, k % NC) for k in range(NZ * NC)]
    up = [(zz * NC + cc, zz * NC + cc + 1) for zz, cc in grid if cc < NC - 1]
    down = [(b, a) for a, b in up]

    row = lax.broadcasted_iota(jnp.int32, (256, 256), 0)
    col = lax.broadcasted_iota(jnp.int32, (256, 256), 1)
    perm = ((row // 32 == col % 8) & (row % 32 == col // 8)).astype(jnp.bfloat16)
    own_mask = lax.dynamic_slice(aux_mask, (0, c * 8), (4, 8)).astype(jnp.float32)
    mask_of = lambda *blocks: jnp.stack([own_mask[:, b] for b in blocks], axis=1)

    e = jnp.arange(BAND, dtype=jnp.int32) - 2
    low, high = blk + jnp.minimum(e, 0), blk + jnp.maximum(e, 0)
    hits = (pair_list[:, 0][:, None] == low[None]) & (pair_list[:, 1][:, None] == high[None])
    scale = jnp.repeat(jnp.sum(hits.astype(jnp.float32), axis=0), BS)

    def spread(blocks, source):
        got = lax.all_to_all(cut_chunk(source, blocks), "blk", split_axis=0, concat_axis=0, tiled=True)
        return got.reshape(4096, BS * len(blocks))

    rows = spread(FIRST, integrals)
    last = spread(LAST, integrals)
    f0, f7 = fit_chunk(rows, 0, perm, metric, mask_of(0, 7))
    above = lax.ppermute(f0, "blk", down)
    below = lax.ppermute(f7, "blk", up)
    f1, f2 = fit_chunk(rows, 1, perm, metric, mask_of(1, 2))
    f5, f6 = fit_chunk(rows, 2, perm, metric, mask_of(5, 6))

    early, *sent = early_tiles(y, (f0, f1, f2, f5, f6, f7))
    early = early_sum(early, over_domains(sent))
    to_below, to_above, edges = edge_tiles(below, f0, f1, f6, f7, above)
    from_above = lax.ppermute(to_below, "blk", down)
    from_below = lax.ppermute(to_above, "blk", up)
    early, from_above, from_below, last = lax.optimization_barrier((early, from_above, from_below, last))

    late, *sent = late_tiles(y, mask_of(3, 4), last, f1, f2, f5, f6, perm, metric, from_below, from_above, edges)
    own, sent = merge(jnp.full((1,), z % 2, jnp.int32), early, late, over_domains(sent))
    got = lax.ppermute(sent, "blk", [(zz * NC + cc, (zz ^ 1) * NC + cc) for zz, cc in grid])
    total, *sent = settle(jnp.full((1,), z // 2, jnp.int32), own, got)
    for j, s in enumerate(sent, 1):
        total = total + lax.ppermute(s, "blk", [(zz * NC + cc, (zz + 2 * j) % NZ * NC + cc) for zz, cc in grid])
    total = lax.ppermute(total, "blk", [(zz * NC + cc, cc * NC + zz) for zz, cc in grid])
    return (total * scale[None, :])[None]


def solution(mesh):
    return jax.shard_map(
        local,
        mesh=mesh,
        in_specs=(P(("aux", "blk"), None, None), P("aux", None), P(), P("aux", None)),
        out_specs=P("blk", "aux", None),
        check_vma=False,
    )
```

```python
import jax
import jax.numpy as jnp
from jax import lax
from jax.experimental import pallas as pl
from jax.experimental.pallas import tpu as pltpu
from jax.sharding import PartitionSpec as P

BS = 128
QB = 128
NZ = 8
NC = 8
NY = 4
PAIR = 2 * BS
BAND = 5
PART = BS // NY
FIRST = (0, 7, 1, 2, 5, 6)
LAST = (3, 4)
VMEM = pltpu.MemorySpace.VMEM
SMEM = pltpu.MemorySpace.SMEM

EARLY_PRODUCTS = (((0, 1), (0, 1, 2)), ((6, 7), (5, 6, 7)), ((2, 5), (2, 5)))
LATE_PRODUCT = ((3, 4), (1, 2, 3, 4, 5, 6))


def tiles_of(products):
    found = {}
    for n, (rows, cols) in enumerate(products):
        for s, r in enumerate(rows):
            for t, k in enumerate(cols):
                if abs(k - r) <= 2:
                    found[r, k - r] = (n, s, t, False)
    for n, (rows, cols) in enumerate(products):
        for s, r in enumerate(rows):
            for t, k in enumerate(cols):
                if abs(k - r) <= 2 and 0 <= k < NC and (k, r - k) not in found:
                    found[k, r - k] = (n, s, t, True)
    return found


EARLY_TILES = tiles_of(EARLY_PRODUCTS)
LATE_TILES = tiles_of((LATE_PRODUCT,))
STRANGE = ((0, -2), (7, 2), (0, -1), (1, -2), (6, 2), (7, 1))


def ordered(slots):
    off = [k for k in slots if k[1] != 0]
    return off + [k for k in slots if k[1] == 0], len(off)


def of_parity(slots, odd):
    return ordered([k for k in slots if k[0] % 2 == odd])[0]


EARLY, EARLY_OFF = ordered(EARLY_TILES)
EARLY_BY = [of_parity(EARLY, odd) for odd in range(2)]
LATE_ALL = STRANGE + tuple(LATE_TILES)
LATE_BY = [of_parity(LATE_ALL, odd) for odd in range(2)]
EARLY_HALF = len(EARLY_BY[0])
LATE_HALF = len(LATE_BY[0])
LATE_DIAGONALS = 1
EARLY_DIAGONALS = 3
AXES = ("aux", "blk")


def sent_slots(slots, off):
    return 2 * len(slots) - off


def runs(blocks):
    found = []
    for n, b in enumerate(blocks):
        if found and found[-1][0] + found[-1][2] == b * BS:
            found[-1][2] += BS
        else:
            found.append([b * BS, n * BS, BS])
    return found


def cut_kernel(source, out_ref, held, sems, *, blocks):
    half = NZ * NC // 2

    def gather(part):
        def one(n, carry):
            k = part * half + n
            z, c = k // NC, k % NC
            for start, at, width in runs(blocks):
                begin = pl.multiple_of(c * 1024 + start, BS)
                pltpu.make_async_copy(
                    source.at[:, z, :, pl.ds(begin, width)], held.at[k, :, :, pl.ds(at, width)], sems.at[part]
                ).start()
            return carry

        lax.fori_loop(0, half, one, 0)

    gather(0)
    gather(1)
    writes = []
    for part in range(2):
        here = held.at[pl.ds(part * half, half)]
        pltpu.make_async_copy(here, here, sems.at[part]).wait()
        write = pltpu.make_async_copy(here, out_ref.at[pl.ds(part * half, half)], sems.at[2 + part])
        write.start()
        writes.append(write)
    for write in writes:
        write.wait()


def cut_chunk(integrals, blocks):
    shape = (NZ * NC, 8, 8, BS * len(blocks))
    return pl.pallas_call(
        lambda *refs: cut_kernel(*refs, blocks=blocks),
        out_shape=jax.ShapeDtypeStruct(shape, jnp.bfloat16),
        in_specs=[pl.BlockSpec(memory_space=pl.ANY)],
        out_specs=pl.BlockSpec(memory_space=pl.ANY),
        scratch_shapes=[pltpu.VMEM(shape, jnp.bfloat16), pltpu.SemaphoreType.DMA((4,))],
        compiler_params=pltpu.CompilerParams(vmem_limit_bytes=60 << 20),
        cost_estimate=pl.CostEstimate(flops=0, bytes_accessed=2 * 8192 * shape[3], transcendentals=0),
        name="cut_chunk",
    )(integrals.reshape(8, NZ, 8, NC * 1024))


def turn_rows(rows_ref, perm_ref, turned_ref, first, count):
    def turn(g, carry):
        start = pl.multiple_of(g * 256, 256)
        turned = jnp.dot(perm_ref[...], rows_ref[pl.ds(start, 256), :], preferred_element_type=jnp.float32)
        turned = turned.astype(jnp.bfloat16)
        at = pl.multiple_of(g * 32, 32)
        for i in range(8):
            turned_ref[i, pl.ds(at, 32), :] = turned[i * 32 : (i + 1) * 32]
        return carry

    lax.fori_loop(first, first + count, turn, 0, unroll=4)


def fit_one(metric_ref, turned_ref, mask_ref, i):
    fitted = jnp.dot(metric_ref[...], turned_ref[i], preferred_element_type=jnp.float32)
    out = []
    for b in range(2):
        column = fitted[:, b * BS : (b + 1) * BS]
        pieces = [column[q * QB : (q + 1) * QB] * mask_ref[q, b] for q in range(4)]
        out.append(jnp.concatenate(pieces, axis=0).astype(jnp.bfloat16))
    return out


def fit_kernel(rows_ref, perm_ref, metric_ref, mask_ref, out_a, out_b, turned_ref):
    turn_rows(rows_ref, perm_ref, turned_ref, 0, 16)

    def fit(i, carry):
        at = pl.multiple_of(i * 512, 512)
        out_a[pl.ds(at, 512), :], out_b[pl.ds(at, 512), :] = fit_one(metric_ref, turned_ref, mask_ref, i)
        return carry

    lax.fori_loop(0, 8, fit, 0, unroll=2)


def whole(shape, at=None):
    return pl.BlockSpec(shape, lambda g: at or (0,) * len(shape))


def fit_chunk(rows, at, perm, metric, mask):
    return pl.pallas_call(
        fit_kernel,
        grid=(1,),
        out_shape=[jax.ShapeDtypeStruct((4096, BS), jnp.bfloat16)] * 2,
        in_specs=[
            whole((4096, PAIR), (0, at)),
            whole((256, 256)),
            whole((512, 512)),
            pl.BlockSpec(memory_space=SMEM),
        ],
        out_specs=[whole((4096, BS))] * 2,
        scratch_shapes=[pltpu.VMEM((8, 512, PAIR), jnp.bfloat16)],
        compiler_params=pltpu.CompilerParams(vmem_limit_bytes=24 << 20),
        cost_estimate=pl.CostEstimate(flops=2 * 4096 * PAIR * 768, bytes_accessed=4 * 4096 * PAIR, transcendentals=0),
        name="fit_chunk",
    )(rows, perm, metric, mask)


def quarter(tile_ref, row, col, which):
    at = pl.multiple_of(row * BS + lax.rem(which, NY) * PART, PART)
    return tile_ref[pl.ds(at, PART), col * BS : (col + 1) * BS]


def put_sent(out_ref, n, low_at, value):
    high = value.astype(jnp.bfloat16)
    out_ref[n] = high
    if low_at is not None:
        out_ref[low_at] = (value - high.astype(jnp.float32)).astype(jnp.bfloat16)


def put_slot(tile_ref, row, col, n, diagonal, slots, off, y, own_ref, out_refs):
    for d in range(NY):
        at = pl.multiple_of(row * BS + lax.rem(y + d, NY) * PART, PART)
        piece = tile_ref[pl.ds(at, PART), col * BS : (col + 1) * BS]
        if d == 0:
            own_ref[n] = piece
            continue
        high = piece.astype(jnp.bfloat16)
        out_refs[d - 1][n] = high
        if diagonal:
            out_refs[d - 1][n + len(slots) - off] = (piece - high.astype(jnp.float32)).astype(jnp.bfloat16)


def put_tiles(found, tiles, flip_ref, slots, off, y, own_ref, out_refs):
    flips = 0
    for r, e in slots:
        if (r, e) not in found:
            continue
        product, s, t, turned = found[r, e]
        n = slots.index((r, e))
        if not turned:
            put_slot(tiles[product], s, t, n, e == 0, slots, off, y, own_ref, out_refs)
            continue
        flip_ref[flips] = tiles[product][s * BS : (s + 1) * BS, t * BS : (t + 1) * BS].T
        put_slot(flip_ref.at[flips], 0, 0, n, False, slots, off, y, own_ref, out_refs)
        flips += 1


EARLY_BLOCKS = (0, 1, 2, 5, 6, 7)


def early_kernel(y_ref, *refs):
    blocks = dict(zip(EARLY_BLOCKS, refs[:6]))
    own_ref, o1, o2, o3, t0, t1, t2, flip_ref = refs[6:]
    tiles = (t0, t1, t2)
    for n, (rows, cols) in enumerate(EARLY_PRODUCTS):
        left = jnp.concatenate([blocks[r][...] for r in rows], axis=1).T
        right = jnp.concatenate([blocks[k][...] for k in cols], axis=1)
        tiles[n][...] = jnp.dot(left, right, preferred_element_type=jnp.float32)
    put_tiles(EARLY_TILES, tiles, flip_ref, EARLY, EARLY_OFF, y_ref[0], own_ref, (o1, o2, o3))


def edge_kernel(below, f0, f1, f6, f7, above, down_ref, up_ref, own_ref):
    low = jnp.dot(
        below[...].T, jnp.concatenate([f0[...], f1[...]], axis=1), preferred_element_type=jnp.float32
    )
    high = jnp.dot(
        above[...].T, jnp.concatenate([f6[...], f7[...]], axis=1), preferred_element_type=jnp.float32
    )
    down_ref[...] = low[:, BS:]
    up_ref[...] = high[:, :BS]
    own_ref[0] = low[:, :BS].T
    own_ref[1] = low[:, BS:].T
    own_ref[2] = high[:, :BS].T
    own_ref[3] = high[:, BS:].T


def edge_tiles(below, f0, f1, f6, f7, above):
    tile = jax.ShapeDtypeStruct((BS, BS), jnp.float32)
    return pl.pallas_call(
        edge_kernel,
        out_shape=[tile, tile, jax.ShapeDtypeStruct((4, BS, BS), jnp.float32)],
        in_specs=[pl.BlockSpec(memory_space=VMEM)] * 6,
        out_specs=[pl.BlockSpec(memory_space=VMEM)] * 3,
        compiler_params=pltpu.CompilerParams(vmem_limit_bytes=24 << 20),
        cost_estimate=pl.CostEstimate(flops=2 * 4096 * 256 * 256, bytes_accessed=6 << 20, transcendentals=0),
        name="edge_tiles",
    )(below, f0, f1, f6, f7, above)


def late_kernel(y_ref, mask_ref, rows_hbm, f1_hbm, f2_hbm, f5_hbm, f6_hbm, perm_ref, metric_ref, from_below, from_above, edges, own_ref, *rest):
    outs, (rows_ref, turned_ref, left_ref, right_ref, tiles_ref, flip_ref, row_sems, sems) = rest[:7], rest[7:]
    feeds = []
    for n in range(4):
        piece = pl.ds(n * 1024, 1024)
        feeds.append(pltpu.make_async_copy(rows_hbm.at[piece], rows_ref.at[piece], row_sems.at[n]))
    fits = [
        pltpu.make_async_copy(f, right_ref.at[n], sems.at[n]) for n, f in enumerate((f1_hbm, f2_hbm, f5_hbm, f6_hbm))
    ]
    for copy in feeds + fits:
        copy.start()
    for n, feed in enumerate(feeds):
        feed.wait()
        turn_rows(rows_ref, perm_ref, turned_ref, 4 * n, 4)

    def step(i, carry):
        at = pl.ds(pl.multiple_of(i * 512, 512), 512)
        left_ref[at, :BS], left_ref[at, BS:] = fit_one(metric_ref, turned_ref, mask_ref, i)
        return carry

    lax.fori_loop(0, 8, step, 0, unroll=2)
    for copy in fits:
        copy.wait()
    f1, f2, f5, f6 = [right_ref[n] for n in range(4)]
    right = jnp.concatenate([f1, f2, left_ref[...], f5, f6], axis=1)
    tiles_ref[...] = jnp.dot(left_ref[...].T, right, preferred_element_type=jnp.float32)
    at = {(0, -2): (from_below, 0, 0), (7, 2): (from_above, 0, 0)}
    for n, slot in enumerate(STRANGE[2:]):
        at[slot] = (edges.at[n], 0, 0)
    flips = 0
    for slot, (_, s, t, turned) in LATE_TILES.items():
        if turned:
            flip_ref[flips] = tiles_ref[s * BS : (s + 1) * BS, t * BS : (t + 1) * BS].T
            at[slot] = (flip_ref.at[flips], 0, 0)
            flips += 1
        else:
            at[slot] = (tiles_ref, s, t)
    y, odd = y_ref[0], y_ref[1]
    for n in range(LATE_HALF):
        for d in range(NY):
            even_piece, odd_piece = [quarter(*at[LATE_BY[k][n]], y + d) for k in range(2)]
            mine = jnp.where(odd == 0, even_piece, odd_piece)
            theirs = jnp.where(odd == 0, odd_piece, even_piece)
            low_at = n + LATE_DIAGONALS if n >= LATE_HALF - LATE_DIAGONALS else None
            if d == 0:
                own_ref[n] = mine
            else:
                put_sent(outs[d - 1], n, low_at, mine)
            put_sent(outs[3 + d], n, low_at, theirs)


def exchange_shapes(slots, off):
    sent = jax.ShapeDtypeStruct((sent_slots(slots, off), PART, BS), jnp.bfloat16)
    return [jax.ShapeDtypeStruct((len(slots), PART, BS), jnp.float32)] + [sent] * 3


def early_tiles(y, blocks):
    return pl.pallas_call(
        early_kernel,
        out_shape=exchange_shapes(EARLY, EARLY_OFF),
        in_specs=[pl.BlockSpec(memory_space=SMEM)] + [pl.BlockSpec(memory_space=VMEM)] * 6,
        out_specs=[pl.BlockSpec(memory_space=VMEM)] * 4,
        scratch_shapes=[
            pltpu.VMEM((PAIR, 3 * BS), jnp.float32),
            pltpu.VMEM((PAIR, 3 * BS), jnp.float32),
            pltpu.VMEM((PAIR, PAIR), jnp.float32),
            pltpu.VMEM((4, BS, BS), jnp.float32),
        ],
        compiler_params=pltpu.CompilerParams(vmem_limit_bytes=40 << 20),
        cost_estimate=pl.CostEstimate(flops=2 * 4096 * 256 * 1024, bytes_accessed=7 << 20, transcendentals=0),
        name="early_tiles",
    )(y, *blocks)


def late_tiles(y, mask, rows, f1, f2, f5, f6, perm, metric, from_below, from_above, edges):
    return pl.pallas_call(
        late_kernel,
        out_shape=[jax.ShapeDtypeStruct((LATE_HALF, PART, BS), jnp.float32)]
        + [jax.ShapeDtypeStruct((LATE_HALF + LATE_DIAGONALS, PART, BS), jnp.bfloat16)] * 7,
        in_specs=[pl.BlockSpec(memory_space=SMEM)] * 2
        + [pl.BlockSpec(memory_space=pl.ANY)] * 5
        + [pl.BlockSpec(memory_space=VMEM)] * 5,
        out_specs=[pl.BlockSpec(memory_space=VMEM)] * 8,
        scratch_shapes=[
            pltpu.VMEM((4096, PAIR), jnp.bfloat16),
            pltpu.VMEM((8, 512, PAIR), jnp.bfloat16),
            pltpu.VMEM((4096, PAIR), jnp.bfloat16),
            pltpu.VMEM((4, 4096, BS), jnp.bfloat16),
            pltpu.VMEM((PAIR, 6 * BS), jnp.float32),
            pltpu.VMEM((6, BS, BS), jnp.float32),
            pltpu.SemaphoreType.DMA((4,)),
            pltpu.SemaphoreType.DMA((4,)),
        ],
        compiler_params=pltpu.CompilerParams(vmem_limit_bytes=52 << 20),
        cost_estimate=pl.CostEstimate(flops=2 * 4096 * 256 * 1536, bytes_accessed=8 << 20, transcendentals=0),
        name="late_tiles",
    )(y, mask, rows, f1, f2, f5, f6, perm, metric, from_below, from_above, edges)


def over_domains(sent):
    return [lax.ppermute(s, "aux", [(a, (a + d) % NY) for a in range(NY)]) for d, s in enumerate(sent, 1)]


def gathered(own_ref, got_refs, n, low_at):
    value = own_ref[n]
    for got in got_refs:
        value = value + got[n].astype(jnp.float32)
        if low_at is not None:
            value = value + got[low_at].astype(jnp.float32)
    return value


def early_sum_kernel(odd_ref, own_ref, g1, g2, g3, mine_ref, theirs_ref):
    odd = odd_ref[0]
    for n in range(EARLY_HALF):
        pair = []
        for k in range(2):
            r, e = EARLY_BY[k][n]
            m = EARLY.index((r, e))
            pair.append(gathered(own_ref, (g1, g2, g3), m, m + len(EARLY) - EARLY_OFF if e == 0 else None))
        low_at = n + EARLY_DIAGONALS if n >= EARLY_HALF - EARLY_DIAGONALS else None
        mine_ref[n] = jnp.where(odd == 0, pair[0], pair[1])
        put_sent(theirs_ref, n, low_at, jnp.where(odd == 0, pair[1], pair[0]))


def early_sum(odd, own, got):
    return pl.pallas_call(
        early_sum_kernel,
        out_shape=[
            jax.ShapeDtypeStruct((EARLY_HALF, PART, BS), jnp.float32),
            jax.ShapeDtypeStruct((EARLY_HALF + EARLY_DIAGONALS, PART, BS), jnp.bfloat16),
        ],
        in_specs=[pl.BlockSpec(memory_space=SMEM)] + [pl.BlockSpec(memory_space=VMEM)] * 4,
        out_specs=[pl.BlockSpec(memory_space=VMEM)] * 2,
        compiler_params=pltpu.CompilerParams(vmem_limit_bytes=16 << 20),
        name="early_sum",
    )(odd, own, *got)


def settle_kernel(z_ref, early_ref, early_got, late_ref, *rest):
    late_got, (own_ref, o1, o2, o3, band_ref) = rest[:7], rest[7:]
    odd, half = lax.rem(z_ref[0], 2), lax.div(z_ref[0], 2)

    def place(by, n, value):
        (r0, e0), (r1, e1) = by[0][n], by[1][n]
        band_ref[jnp.where(odd == 0, r0 // 2, r1 // 2), jnp.where(odd == 0, e0 + 2, e1 + 2)] = value

    for n in range(EARLY_HALF):
        low_at = n + EARLY_DIAGONALS if n >= EARLY_HALF - EARLY_DIAGONALS else None
        place(EARLY_BY, n, gathered(early_ref, (early_got,), n, low_at))
    for n in range(LATE_HALF):
        low_at = n + LATE_DIAGONALS if n >= LATE_HALF - LATE_DIAGONALS else None
        place(LATE_BY, n, gathered(late_ref, late_got, n, low_at))
    for j, out in enumerate((own_ref, o1, o2, o3)):
        k = lax.rem(half + j, 4)
        for slot in range(BAND):
            if j == 0:
                out[:, slot * BS : (slot + 1) * BS] = band_ref[k, slot]
            else:
                put_sent(out, slot, BAND if slot == 2 else None, band_ref[k, slot])


def settle(z, early, early_got, late, late_got):
    return pl.pallas_call(
        settle_kernel,
        out_shape=[jax.ShapeDtypeStruct((PART, BAND * BS), jnp.float32)]
        + [jax.ShapeDtypeStruct((BAND + 1, PART, BS), jnp.bfloat16)] * 3,
        in_specs=[pl.BlockSpec(memory_space=SMEM)] + [pl.BlockSpec(memory_space=VMEM)] * 10,
        out_specs=[pl.BlockSpec(memory_space=VMEM)] * 4,
        scratch_shapes=[pltpu.VMEM((4, BAND, PART, BS), jnp.float32)],
        compiler_params=pltpu.CompilerParams(vmem_limit_bytes=16 << 20),
        name="settle",
    )(z, early, early_got, late, *late_got)


def finish_kernel(own_ref, g1, g2, g3, out_ref):
    for slot in range(BAND):
        value = own_ref[:, slot * BS : (slot + 1) * BS]
        for got in (g1, g2, g3):
            value = value + got[slot].astype(jnp.float32)
            if slot == 2:
                value = value + got[BAND].astype(jnp.float32)
        out_ref[:, slot * BS : (slot + 1) * BS] = value


def finish(own, got):
    return pl.pallas_call(
        finish_kernel,
        out_shape=jax.ShapeDtypeStruct((PART, BAND * BS), jnp.float32),
        in_specs=[pl.BlockSpec(memory_space=VMEM)] * 4,
        out_specs=pl.BlockSpec(memory_space=VMEM),
        compiler_params=pltpu.CompilerParams(vmem_limit_bytes=16 << 20),
        name="finish",
    )(own, *got)


def local(integrals, metric, pair_list, aux_mask):
    blk = lax.axis_index("blk")
    z, c = blk // NC, blk % NC
    y = jnp.stack([lax.axis_index("aux"), z % 2]).astype(jnp.int32)
    at_z = jnp.full((1,), z, jnp.int32)
    grid = [(k // NC, k % NC) for k in range(NZ * NC)]
    up = [(zz * NC + cc, zz * NC + cc + 1) for zz, cc in grid if cc < NC - 1]
    down = [(b, a) for a, b in up]

    row = lax.broadcasted_iota(jnp.int32, (256, 256), 0)
    col = lax.broadcasted_iota(jnp.int32, (256, 256), 1)
    perm = ((row // 32 == col % 8) & (row % 32 == col // 8)).astype(jnp.bfloat16)
    own_mask = lax.dynamic_slice(aux_mask, (0, c * 8), (4, 8)).astype(jnp.float32)
    mask_of = lambda *blocks: jnp.stack([own_mask[:, b] for b in blocks], axis=1)

    e = jnp.arange(BAND, dtype=jnp.int32) - 2
    low, high = blk + jnp.minimum(e, 0), blk + jnp.maximum(e, 0)
    hits = (pair_list[:, 0][:, None] == low[None]) & (pair_list[:, 1][:, None] == high[None])
    scale = jnp.repeat(jnp.sum(hits.astype(jnp.float32), axis=0), BS)

    def spread(blocks, source):
        got = lax.all_to_all(cut_chunk(source, blocks), "blk", split_axis=0, concat_axis=0, tiled=True)
        return got.reshape(4096, BS * len(blocks))

    rows = spread(FIRST, integrals)
    last = spread(LAST, integrals)
    f0, f7 = fit_chunk(rows, 0, perm, metric, mask_of(0, 7))
    above = lax.ppermute(f0, "blk", down)
    below = lax.ppermute(f7, "blk", up)
    f1, f2 = fit_chunk(rows, 1, perm, metric, mask_of(1, 2))
    f5, f6 = fit_chunk(rows, 2, perm, metric, mask_of(5, 6))

    early, *sent = early_tiles(y, (f0, f1, f2, f5, f6, f7))
    early, early_sent = early_sum(jnp.full((1,), z % 2, jnp.int32), early, over_domains(sent))
    to_below, to_above, edges = edge_tiles(below, f0, f1, f6, f7, above)
    from_above = lax.ppermute(to_below, "blk", down)
    from_below = lax.ppermute(to_above, "blk", up)
    early_sent, from_above, from_below, last = lax.optimization_barrier((early_sent, from_above, from_below, last))

    late, *sent = late_tiles(y, mask_of(3, 4), last, f1, f2, f5, f6, perm, metric, from_below, from_above, edges)
    whole_grid = [(a, zz, cc) for a in range(NY) for zz, cc in grid]

    def move(array, d, flip):
        pairs = [
            (a * NZ * NC + zz * NC + cc, (a + d) % NY * NZ * NC + (zz ^ flip) * NC + cc) for a, zz, cc in whole_grid
        ]
        return lax.ppermute(array, AXES, pairs)

    early_got = move(early_sent, 0, 1)
    late_got = [move(s, d, 0) for d, s in enumerate(sent[:3], 1)] + [move(s, d, 1) for d, s in enumerate(sent[3:])]
    own, *sent = settle(at_z, early, early_got, late, late_got)
    got = [
        lax.ppermute(s, "blk", [(zz * NC + cc, (zz + 2 * j) % NZ * NC + cc) for zz, cc in grid])
        for j, s in enumerate(sent, 1)
    ]
    total = lax.ppermute(finish(own, got), "blk", [(zz * NC + cc, cc * NC + zz) for zz, cc in grid])
    return (total * scale[None, :])[None]


def solution(mesh):
    return jax.shard_map(
        local,
        mesh=mesh,
        in_specs=(P(("aux", "blk"), None, None), P("aux", None), P(), P("aux", None)),
        out_specs=P("blk", "aux", None),
        check_vma=False,
    )
```

```python
import jax
import jax.numpy as jnp
from jax import lax
from jax.experimental import pallas as pl
from jax.experimental.pallas import tpu as pltpu
from jax.sharding import PartitionSpec as P

BS = 128
QB = 128
NZ = 8
NC = 8
NY = 4
PAIR = 2 * BS
BAND = 5
PART = BS // NY
PARTS = 2
FIRST = (0, 7, 1, 2, 5, 6)
LAST = (3, 4)
VMEM = pltpu.MemorySpace.VMEM
SMEM = pltpu.MemorySpace.SMEM

EARLY_PRODUCTS = (((0, 1), (0, 1, 2)), ((6, 7), (5, 6, 7)), ((2, 5), (2, 5)))
LATE_PRODUCT = ((3, 4), (1, 2, 3, 4, 5, 6))


def tiles_of(products):
    found = {}
    for n, (rows, cols) in enumerate(products):
        for s, r in enumerate(rows):
            for t, k in enumerate(cols):
                if abs(k - r) <= 2:
                    found[r, k - r] = (n, s, t, False)
    for n, (rows, cols) in enumerate(products):
        for s, r in enumerate(rows):
            for t, k in enumerate(cols):
                if abs(k - r) <= 2 and 0 <= k < NC and (k, r - k) not in found:
                    found[k, r - k] = (n, s, t, True)
    return found


EARLY_TILES = tiles_of(EARLY_PRODUCTS)
LATE_TILES = tiles_of((LATE_PRODUCT,))
STRANGE = ((0, -2), (7, 2), (0, -1), (1, -2), (6, 2), (7, 1))


def ordered(slots):
    off = [k for k in slots if k[1] != 0]
    return off + [k for k in slots if k[1] == 0], len(off)


def of_parity(slots, odd):
    return ordered([k for k in slots if k[0] % 2 == odd])[0]


EARLY, EARLY_OFF = ordered(EARLY_TILES)
EARLY_BY = [of_parity(EARLY, odd) for odd in range(2)]
LATE_ALL = STRANGE + tuple(LATE_TILES)
LATE_BY = [of_parity(LATE_ALL, odd) for odd in range(2)]
EARLY_HALF = len(EARLY_BY[0])
LATE_HALF = len(LATE_BY[0])
LATE_DIAGONALS = 1
EARLY_DIAGONALS = 3
AXES = ("aux", "blk")


def sent_slots(slots, off):
    return 2 * len(slots) - off


def runs(blocks):
    found = []
    for n, b in enumerate(blocks):
        if found and found[-1][0] + found[-1][2] == b * BS:
            found[-1][2] += BS
        else:
            found.append([b * BS, n * BS, BS])
    return found


def cut_kernel(source, out_ref, held, sems, *, blocks):
    size = NZ * NC // PARTS

    def gather(part):
        def one(n, carry):
            k = part * size + n
            z, c = k // NC, k % NC
            for start, at, width in runs(blocks):
                begin = pl.multiple_of(c * 1024 + start, BS)
                pltpu.make_async_copy(
                    source.at[:, z, :, pl.ds(begin, width)], held.at[k, :, :, pl.ds(at, width)], sems.at[part]
                ).start()
            return carry

        lax.fori_loop(0, size, one, 0)

    for part in range(PARTS):
        gather(part)
    writes = []
    for part in range(PARTS):
        here = held.at[pl.ds(part * size, size)]
        pltpu.make_async_copy(here, here, sems.at[part]).wait()
        write = pltpu.make_async_copy(here, out_ref.at[pl.ds(part * size, size)], sems.at[PARTS + part])
        write.start()
        writes.append(write)
    for write in writes:
        write.wait()


def cut_chunk(integrals, blocks):
    shape = (NZ * NC, 8, 8, BS * len(blocks))
    return pl.pallas_call(
        lambda *refs: cut_kernel(*refs, blocks=blocks),
        out_shape=jax.ShapeDtypeStruct(shape, jnp.bfloat16),
        in_specs=[pl.BlockSpec(memory_space=pl.ANY)],
        out_specs=pl.BlockSpec(memory_space=pl.ANY),
        scratch_shapes=[pltpu.VMEM(shape, jnp.bfloat16), pltpu.SemaphoreType.DMA((2 * PARTS,))],
        compiler_params=pltpu.CompilerParams(vmem_limit_bytes=60 << 20),
        cost_estimate=pl.CostEstimate(flops=0, bytes_accessed=2 * 8192 * shape[3], transcendentals=0),
        name="cut_chunk",
    )(integrals.reshape(8, NZ, 8, NC * 1024))


def turn_rows(rows_refs, perm_ref, turned_ref, first, count):
    def turn(g, carry):
        start = pl.multiple_of(g * 256, 256)
        rows = jnp.concatenate([rows_ref[pl.ds(start, 256), :] for rows_ref in rows_refs], axis=1)
        turned = jnp.dot(perm_ref[...], rows, preferred_element_type=jnp.float32)
        turned = turned.astype(jnp.bfloat16)
        at = pl.multiple_of(g * 32, 32)
        for i in range(8):
            turned_ref[i, pl.ds(at, 32), :] = turned[i * 32 : (i + 1) * 32]
        return carry

    lax.fori_loop(first, first + count, turn, 0, unroll=4)


def fit_one(metric_ref, turned_ref, mask_ref, i):
    fitted = jnp.dot(metric_ref[...], turned_ref[i], preferred_element_type=jnp.float32)
    out = []
    for b in range(2):
        column = fitted[:, b * BS : (b + 1) * BS]
        pieces = [column[q * QB : (q + 1) * QB] * mask_ref[q, b] for q in range(4)]
        out.append(jnp.concatenate(pieces, axis=0).astype(jnp.bfloat16))
    return out


def fit_kernel(rows_a, rows_b, perm_ref, metric_ref, mask_ref, out_a, out_b, turned_ref):
    turn_rows((rows_a, rows_b), perm_ref, turned_ref, 0, 16)

    def fit(i, carry):
        at = pl.multiple_of(i * 512, 512)
        out_a[pl.ds(at, 512), :], out_b[pl.ds(at, 512), :] = fit_one(metric_ref, turned_ref, mask_ref, i)
        return carry

    lax.fori_loop(0, 8, fit, 0, unroll=2)


def whole(shape, at=None):
    return pl.BlockSpec(shape, lambda g: at or (0,) * len(shape))


def fit_chunk(rows, pair, perm, metric, mask):
    return pl.pallas_call(
        fit_kernel,
        grid=(1,),
        out_shape=[jax.ShapeDtypeStruct((4096, BS), jnp.bfloat16)] * 2,
        in_specs=[
            whole((4096, BS), (0, FIRST.index(pair[0]))),
            whole((4096, BS), (0, FIRST.index(pair[1]))),
            whole((256, 256)),
            whole((512, 512)),
            pl.BlockSpec(memory_space=SMEM),
        ],
        out_specs=[whole((4096, BS))] * 2,
        scratch_shapes=[pltpu.VMEM((8, 512, PAIR), jnp.bfloat16)],
        compiler_params=pltpu.CompilerParams(vmem_limit_bytes=24 << 20),
        cost_estimate=pl.CostEstimate(flops=2 * 4096 * PAIR * 768, bytes_accessed=4 * 4096 * PAIR, transcendentals=0),
        name="fit_chunk",
    )(rows, rows, perm, metric, mask)


def quarter(tile_ref, row, col, which):
    at = pl.multiple_of(row * BS + lax.rem(which, NY) * PART, PART)
    return tile_ref[pl.ds(at, PART), col * BS : (col + 1) * BS]


def put_sent(out_ref, n, low_at, value):
    high = value.astype(jnp.bfloat16)
    out_ref[n] = high
    if low_at is not None:
        out_ref[low_at] = (value - high.astype(jnp.float32)).astype(jnp.bfloat16)


def put_slot(tile_ref, row, col, n, diagonal, slots, off, y, own_ref, out_refs):
    for d in range(NY):
        at = pl.multiple_of(row * BS + lax.rem(y + d, NY) * PART, PART)
        piece = tile_ref[pl.ds(at, PART), col * BS : (col + 1) * BS]
        if d == 0:
            own_ref[n] = piece
            continue
        high = piece.astype(jnp.bfloat16)
        out_refs[d - 1][n] = high
        if diagonal:
            out_refs[d - 1][n + len(slots) - off] = (piece - high.astype(jnp.float32)).astype(jnp.bfloat16)


def put_tiles(found, tiles, flip_ref, slots, off, y, own_ref, out_refs):
    flips = 0
    for r, e in slots:
        if (r, e) not in found:
            continue
        product, s, t, turned = found[r, e]
        n = slots.index((r, e))
        if not turned:
            put_slot(tiles[product], s, t, n, e == 0, slots, off, y, own_ref, out_refs)
            continue
        flip_ref[flips] = tiles[product][s * BS : (s + 1) * BS, t * BS : (t + 1) * BS].T
        put_slot(flip_ref.at[flips], 0, 0, n, False, slots, off, y, own_ref, out_refs)
        flips += 1


EARLY_BLOCKS = (0, 1, 2, 5, 6, 7)


def early_kernel(y_ref, *refs):
    blocks = dict(zip(EARLY_BLOCKS, refs[:6]))
    own_ref, o1, o2, o3, t0, t1, t2, flip_ref = refs[6:]
    tiles = (t0, t1, t2)
    for n, (rows, cols) in enumerate(EARLY_PRODUCTS):
        left = jnp.concatenate([blocks[r][...] for r in rows], axis=1).T
        right = jnp.concatenate([blocks[k][...] for k in cols], axis=1)
        tiles[n][...] = jnp.dot(left, right, preferred_element_type=jnp.float32)
    put_tiles(EARLY_TILES, tiles, flip_ref, EARLY, EARLY_OFF, y_ref[0], own_ref, (o1, o2, o3))


def edge_kernel(below, f0, f1, f6, f7, above, down_ref, up_ref, own_ref):
    low = jnp.dot(
        below[...].T, jnp.concatenate([f0[...], f1[...]], axis=1), preferred_element_type=jnp.float32
    )
    high = jnp.dot(
        above[...].T, jnp.concatenate([f6[...], f7[...]], axis=1), preferred_element_type=jnp.float32
    )
    down_ref[...] = low[:, BS:]
    up_ref[...] = high[:, :BS]
    own_ref[0] = low[:, :BS].T
    own_ref[1] = low[:, BS:].T
    own_ref[2] = high[:, :BS].T
    own_ref[3] = high[:, BS:].T


def edge_tiles(below, f0, f1, f6, f7, above):
    tile = jax.ShapeDtypeStruct((BS, BS), jnp.float32)
    return pl.pallas_call(
        edge_kernel,
        out_shape=[tile, tile, jax.ShapeDtypeStruct((4, BS, BS), jnp.float32)],
        in_specs=[pl.BlockSpec(memory_space=VMEM)] * 6,
        out_specs=[pl.BlockSpec(memory_space=VMEM)] * 3,
        compiler_params=pltpu.CompilerParams(vmem_limit_bytes=24 << 20),
        cost_estimate=pl.CostEstimate(flops=2 * 4096 * 256 * 256, bytes_accessed=6 << 20, transcendentals=0),
        name="edge_tiles",
    )(below, f0, f1, f6, f7, above)


def late_kernel(y_ref, mask_ref, rows_hbm, f1_hbm, f2_hbm, f5_hbm, f6_hbm, perm_ref, metric_ref, from_below, from_above, edges, own_ref, *rest):
    outs, (rows_ref, turned_ref, left_ref, right_ref, tiles_ref, flip_ref, row_sems, sems) = rest[:7], rest[7:]
    feeds = []
    for n in range(4):
        piece = pl.ds(n * 1024, 1024)
        feeds.append(pltpu.make_async_copy(rows_hbm.at[piece], rows_ref.at[piece], row_sems.at[n]))
    fits = [
        pltpu.make_async_copy(f, right_ref.at[n], sems.at[n]) for n, f in enumerate((f1_hbm, f2_hbm, f5_hbm, f6_hbm))
    ]
    for copy in feeds + fits:
        copy.start()
    for n, feed in enumerate(feeds):
        feed.wait()
        turn_rows((rows_ref,), perm_ref, turned_ref, 4 * n, 4)

    def step(i, carry):
        at = pl.ds(pl.multiple_of(i * 512, 512), 512)
        left_ref[at, :BS], left_ref[at, BS:] = fit_one(metric_ref, turned_ref, mask_ref, i)
        return carry

    lax.fori_loop(0, 8, step, 0, unroll=4)
    for copy in fits:
        copy.wait()
    f1, f2, f5, f6 = [right_ref[n] for n in range(4)]
    right = jnp.concatenate([f1, f2, left_ref[...], f5, f6], axis=1)
    tiles_ref[...] = jnp.dot(left_ref[...].T, right, preferred_element_type=jnp.float32)
    at = {(0, -2): (from_below, 0, 0), (7, 2): (from_above, 0, 0)}
    for n, slot in enumerate(STRANGE[2:]):
        at[slot] = (edges.at[n], 0, 0)
    flips = 0
    for slot, (_, s, t, turned) in LATE_TILES.items():
        if turned:
            flip_ref[flips] = tiles_ref[s * BS : (s + 1) * BS, t * BS : (t + 1) * BS].T
            at[slot] = (flip_ref.at[flips], 0, 0)
            flips += 1
        else:
            at[slot] = (tiles_ref, s, t)
    y, odd = y_ref[0], y_ref[1]
    for n in range(LATE_HALF):
        for d in range(NY):
            even_piece, odd_piece = [quarter(*at[LATE_BY[k][n]], y + d) for k in range(2)]
            mine = jnp.where(odd == 0, even_piece, odd_piece)
            theirs = jnp.where(odd == 0, odd_piece, even_piece)
            low_at = n + LATE_DIAGONALS if n >= LATE_HALF - LATE_DIAGONALS else None
            if d == 0:
                own_ref[n] = mine
            else:
                put_sent(outs[d - 1], n, low_at, mine)
            put_sent(outs[3 + d], n, low_at, theirs)


def exchange_shapes(slots, off):
    sent = jax.ShapeDtypeStruct((sent_slots(slots, off), PART, BS), jnp.bfloat16)
    return [jax.ShapeDtypeStruct((len(slots), PART, BS), jnp.float32)] + [sent] * 3


def early_tiles(y, blocks):
    return pl.pallas_call(
        early_kernel,
        out_shape=exchange_shapes(EARLY, EARLY_OFF),
        in_specs=[pl.BlockSpec(memory_space=SMEM)] + [pl.BlockSpec(memory_space=VMEM)] * 6,
        out_specs=[pl.BlockSpec(memory_space=VMEM)] * 4,
        scratch_shapes=[
            pltpu.VMEM((PAIR, 3 * BS), jnp.float32),
            pltpu.VMEM((PAIR, 3 * BS), jnp.float32),
            pltpu.VMEM((PAIR, PAIR), jnp.float32),
            pltpu.VMEM((4, BS, BS), jnp.float32),
        ],
        compiler_params=pltpu.CompilerParams(vmem_limit_bytes=40 << 20),
        cost_estimate=pl.CostEstimate(flops=2 * 4096 * 256 * 1024, bytes_accessed=7 << 20, transcendentals=0),
        name="early_tiles",
    )(y, *blocks)


def late_tiles(y, mask, rows, f1, f2, f5, f6, perm, metric, from_below, from_above, edges):
    return pl.pallas_call(
        late_kernel,
        out_shape=[jax.ShapeDtypeStruct((LATE_HALF, PART, BS), jnp.float32)]
        + [jax.ShapeDtypeStruct((LATE_HALF + LATE_DIAGONALS, PART, BS), jnp.bfloat16)] * 7,
        in_specs=[pl.BlockSpec(memory_space=SMEM)] * 2
        + [pl.BlockSpec(memory_space=pl.ANY)] * 5
        + [pl.BlockSpec(memory_space=VMEM)] * 5,
        out_specs=[pl.BlockSpec(memory_space=VMEM)] * 8,
        scratch_shapes=[
            pltpu.VMEM((4096, PAIR), jnp.bfloat16),
            pltpu.VMEM((8, 512, PAIR), jnp.bfloat16),
            pltpu.VMEM((4096, PAIR), jnp.bfloat16),
            pltpu.VMEM((4, 4096, BS), jnp.bfloat16),
            pltpu.VMEM((PAIR, 6 * BS), jnp.float32),
            pltpu.VMEM((6, BS, BS), jnp.float32),
            pltpu.SemaphoreType.DMA((4,)),
            pltpu.SemaphoreType.DMA((4,)),
        ],
        compiler_params=pltpu.CompilerParams(vmem_limit_bytes=52 << 20),
        cost_estimate=pl.CostEstimate(flops=2 * 4096 * 256 * 1536, bytes_accessed=8 << 20, transcendentals=0),
        name="late_tiles",
    )(y, mask, rows, f1, f2, f5, f6, perm, metric, from_below, from_above, edges)


def over_domains(sent):
    return [lax.ppermute(s, "aux", [(a, (a + d) % NY) for a in range(NY)]) for d, s in enumerate(sent, 1)]


def gathered(own_ref, got_refs, n, low_at):
    value = own_ref[n]
    for got in got_refs:
        value = value + got[n].astype(jnp.float32)
        if low_at is not None:
            value = value + got[low_at].astype(jnp.float32)
    return value


def early_sum_kernel(odd_ref, own_ref, g1, g2, g3, mine_ref, theirs_ref):
    odd = odd_ref[0]
    for n in range(EARLY_HALF):
        pair = []
        for k in range(2):
            r, e = EARLY_BY[k][n]
            m = EARLY.index((r, e))
            pair.append(gathered(own_ref, (g1, g2, g3), m, m + len(EARLY) - EARLY_OFF if e == 0 else None))
        low_at = n + EARLY_DIAGONALS if n >= EARLY_HALF - EARLY_DIAGONALS else None
        mine_ref[n] = jnp.where(odd == 0, pair[0], pair[1])
        put_sent(theirs_ref, n, low_at, jnp.where(odd == 0, pair[1], pair[0]))


def early_sum(odd, own, got):
    return pl.pallas_call(
        early_sum_kernel,
        out_shape=[
            jax.ShapeDtypeStruct((EARLY_HALF, PART, BS), jnp.float32),
            jax.ShapeDtypeStruct((EARLY_HALF + EARLY_DIAGONALS, PART, BS), jnp.bfloat16),
        ],
        in_specs=[pl.BlockSpec(memory_space=SMEM)] + [pl.BlockSpec(memory_space=VMEM)] * 4,
        out_specs=[pl.BlockSpec(memory_space=VMEM)] * 2,
        compiler_params=pltpu.CompilerParams(vmem_limit_bytes=16 << 20),
        name="early_sum",
    )(odd, own, *got)


def settle_kernel(z_ref, early_ref, early_got, late_ref, *rest):
    late_got, (own_ref, o1, o2, o3, band_ref) = rest[:7], rest[7:]
    odd, half = lax.rem(z_ref[0], 2), lax.div(z_ref[0], 2)

    def place(by, n, value):
        (r0, e0), (r1, e1) = by[0][n], by[1][n]
        band_ref[jnp.where(odd == 0, r0 // 2, r1 // 2), jnp.where(odd == 0, e0 + 2, e1 + 2)] = value

    for n in range(EARLY_HALF):
        low_at = n + EARLY_DIAGONALS if n >= EARLY_HALF - EARLY_DIAGONALS else None
        place(EARLY_BY, n, gathered(early_ref, (early_got,), n, low_at))
    for n in range(LATE_HALF):
        low_at = n + LATE_DIAGONALS if n >= LATE_HALF - LATE_DIAGONALS else None
        place(LATE_BY, n, gathered(late_ref, late_got, n, low_at))
    for j, out in enumerate((own_ref, o1, o2, o3)):
        k = lax.rem(half + j, 4)
        for slot in range(BAND):
            out[:, slot * BS : (slot + 1) * BS] = band_ref[k, slot]


def settle(z, early, early_got, late, late_got):
    return pl.pallas_call(
        settle_kernel,
        out_shape=[jax.ShapeDtypeStruct((PART, BAND * BS), jnp.float32)] * 4,
        in_specs=[pl.BlockSpec(memory_space=SMEM)] + [pl.BlockSpec(memory_space=VMEM)] * 10,
        out_specs=[pl.BlockSpec(memory_space=VMEM)] * 4,
        scratch_shapes=[pltpu.VMEM((4, BAND, PART, BS), jnp.float32)],
        compiler_params=pltpu.CompilerParams(vmem_limit_bytes=16 << 20),
        name="settle",
    )(z, early, early_got, late, *late_got)


def local(integrals, metric, pair_list, aux_mask):
    blk = lax.axis_index("blk")
    z, c = blk // NC, blk % NC
    y = jnp.stack([lax.axis_index("aux"), z % 2]).astype(jnp.int32)
    at_z = jnp.full((1,), z, jnp.int32)
    grid = [(k // NC, k % NC) for k in range(NZ * NC)]
    up = [(zz * NC + cc, zz * NC + cc + 1) for zz, cc in grid if cc < NC - 1]
    down = [(b, a) for a, b in up]

    row = lax.broadcasted_iota(jnp.int32, (256, 256), 0)
    col = lax.broadcasted_iota(jnp.int32, (256, 256), 1)
    perm = ((row // 32 == col % 8) & (row % 32 == col // 8)).astype(jnp.bfloat16)
    own_mask = lax.dynamic_slice(aux_mask, (0, c * 8), (4, 8)).astype(jnp.float32)
    mask_of = lambda *blocks: jnp.stack([own_mask[:, b] for b in blocks], axis=1)

    e = jnp.arange(BAND, dtype=jnp.int32) - 2
    home = c * NC + z
    low, high = home + jnp.minimum(e, 0), home + jnp.maximum(e, 0)
    hits = (pair_list[:, 0][:, None] == low[None]) & (pair_list[:, 1][:, None] == high[None])
    scale = jnp.repeat(jnp.sum(hits.astype(jnp.float32), axis=0), BS)

    whole_grid = [(a, zz, cc) for a in range(NY) for zz, cc in grid]

    def move(array, d, flip):
        pairs = [
            (a * NZ * NC + zz * NC + cc, (a + d) % NY * NZ * NC + (zz ^ flip) * NC + cc) for a, zz, cc in whole_grid
        ]
        return lax.ppermute(array, AXES, pairs)

    def spread(blocks, source):
        got = lax.all_to_all(cut_chunk(source, blocks), "blk", split_axis=0, concat_axis=0, tiled=True)
        return got.reshape(4096, BS * len(blocks))

    rows = spread(FIRST, integrals)
    last = spread(LAST, integrals)
    f0, f7 = fit_chunk(rows, (0, 7), perm, metric, mask_of(0, 7))
    above = lax.ppermute(f0, "blk", down)
    below = lax.ppermute(f7, "blk", up)
    f1, f2 = fit_chunk(rows, (1, 2), perm, metric, mask_of(1, 2))
    f5, f6 = fit_chunk(rows, (5, 6), perm, metric, mask_of(5, 6))

    early, *sent = early_tiles(y, (f0, f1, f2, f5, f6, f7))
    early, early_sent = early_sum(jnp.full((1,), z % 2, jnp.int32), early, over_domains(sent))
    to_below, to_above, edges = edge_tiles(below, f0, f1, f6, f7, above)
    from_above = lax.ppermute(to_below, "blk", down)
    from_below = lax.ppermute(to_above, "blk", up)
    early_got = move(early_sent, 0, 1)
    early_got, from_above, from_below, last = lax.optimization_barrier((early_got, from_above, from_below, last))

    late, *sent = late_tiles(y, mask_of(3, 4), last, f1, f2, f5, f6, perm, metric, from_below, from_above, edges)
    late_got = [move(s, d, 0) for d, s in enumerate(sent[:3], 1)] + [move(s, d, 1) for d, s in enumerate(sent[3:])]
    total, *sent = settle(at_z, early, early_got, late, late_got)
    for j, s in enumerate(sent, 1):
        total = total + lax.ppermute(s, "blk", [(zz * NC + cc, (zz + 2 * j) % NZ * NC + cc) for zz, cc in grid])
    total = (total * scale[None, :])[None]
    return lax.ppermute(total, "blk", [(zz * NC + cc, cc * NC + zz) for zz, cc in grid])


def solution(mesh):
    return jax.shard_map(
        local,
        mesh=mesh,
        in_specs=(P(("aux", "blk"), None, None), P("aux", None), P(), P("aux", None)),
        out_specs=P("blk", "aux", None),
        check_vma=False,
    )
```

```python
import jax
import jax.numpy as jnp
from jax import lax
from jax.experimental import pallas as pl
from jax.experimental.pallas import tpu as pltpu
from jax.sharding import PartitionSpec as P

BS = 128
QB = 128
NZ = 8
NC = 8
NY = 4
PAIR = 2 * BS
BAND = 5
PART = BS // NY
PARTS = 2
FIRST = (0, 7, 1, 2, 5, 6)
LAST = (3, 4)
VMEM = pltpu.MemorySpace.VMEM
SMEM = pltpu.MemorySpace.SMEM

EARLY_PRODUCTS = (((0, 1), (0, 1, 2)), ((6, 7), (5, 6, 7)), ((2, 5), (2, 5)))
LATE_PRODUCT = ((3, 4), (1, 2, 3, 4, 5, 6))


def tiles_of(products):
    found = {}
    for n, (rows, cols) in enumerate(products):
        for s, r in enumerate(rows):
            for t, k in enumerate(cols):
                if abs(k - r) <= 2:
                    found[r, k - r] = (n, s, t, False)
    for n, (rows, cols) in enumerate(products):
        for s, r in enumerate(rows):
            for t, k in enumerate(cols):
                if abs(k - r) <= 2 and 0 <= k < NC and (k, r - k) not in found:
                    found[k, r - k] = (n, s, t, True)
    return found


EARLY_TILES = tiles_of(EARLY_PRODUCTS)
LATE_TILES = tiles_of((LATE_PRODUCT,))
STRANGE = ((0, -2), (7, 2), (0, -1), (1, -2), (6, 2), (7, 1))


def ordered(slots):
    off = [k for k in slots if k[1] != 0]
    return off + [k for k in slots if k[1] == 0], len(off)


def of_parity(slots, odd):
    return ordered([k for k in slots if k[0] % 2 == odd])[0]


EARLY, EARLY_OFF = ordered(EARLY_TILES)
EARLY_BY = [of_parity(EARLY, odd) for odd in range(2)]
LATE_ALL = STRANGE + tuple(LATE_TILES)
LATE_BY = [of_parity(LATE_ALL, odd) for odd in range(2)]
EARLY_HALF = len(EARLY_BY[0])
LATE_HALF = len(LATE_BY[0])
LATE_DIAGONALS = 1
EARLY_DIAGONALS = 3
AXES = ("aux", "blk")


def sent_slots(slots, off):
    return 2 * len(slots) - off


def runs(blocks):
    found = []
    for n, b in enumerate(blocks):
        if found and found[-1][0] + found[-1][2] == b * BS:
            found[-1][2] += BS
        else:
            found.append([b * BS, n * BS, BS])
    return found


def cut_kernel(source, out_ref, held, sems, *, blocks):
    size = NZ * NC // PARTS

    def gather(part):
        def one(n, carry):
            k = part * size + n
            z, c = k // NC, k % NC
            for start, at, width in runs(blocks):
                begin = pl.multiple_of(c * 1024 + start, BS)
                pltpu.make_async_copy(
                    source.at[:, z, :, pl.ds(begin, width)], held.at[k, :, :, pl.ds(at, width)], sems.at[part]
                ).start()
            return carry

        lax.fori_loop(0, size, one, 0)

    for part in range(PARTS):
        gather(part)
    writes = []
    for part in range(PARTS):
        here = held.at[pl.ds(part * size, size)]
        pltpu.make_async_copy(here, here, sems.at[part]).wait()
        write = pltpu.make_async_copy(here, out_ref.at[pl.ds(part * size, size)], sems.at[PARTS + part])
        write.start()
        writes.append(write)
    for write in writes:
        write.wait()


def cut_chunk(integrals, blocks):
    shape = (NZ * NC, 8, 8, BS * len(blocks))
    return pl.pallas_call(
        lambda *refs: cut_kernel(*refs, blocks=blocks),
        out_shape=jax.ShapeDtypeStruct(shape, jnp.bfloat16),
        in_specs=[pl.BlockSpec(memory_space=pl.ANY)],
        out_specs=pl.BlockSpec(memory_space=pl.ANY),
        scratch_shapes=[pltpu.VMEM(shape, jnp.bfloat16), pltpu.SemaphoreType.DMA((2 * PARTS,))],
        compiler_params=pltpu.CompilerParams(vmem_limit_bytes=60 << 20),
        cost_estimate=pl.CostEstimate(flops=0, bytes_accessed=2 * 8192 * shape[3], transcendentals=0),
        name="cut_chunk",
    )(integrals.reshape(8, NZ, 8, NC * 1024))


def turn_rows(rows_refs, perm_ref, turned_ref, first, count):
    def turn(g, carry):
        start = pl.multiple_of(g * 256, 256)
        rows = jnp.concatenate([rows_ref[pl.ds(start, 256), :] for rows_ref in rows_refs], axis=1)
        turned = jnp.dot(perm_ref[...], rows, preferred_element_type=jnp.float32)
        turned = turned.astype(jnp.bfloat16)
        at = pl.multiple_of(g * 32, 32)
        for i in range(8):
            turned_ref[i, pl.ds(at, 32), :] = turned[i * 32 : (i + 1) * 32]
        return carry

    lax.fori_loop(first, first + count, turn, 0, unroll=min(count, 8))


def fit_one(metric_ref, turned_ref, mask_ref, i):
    fitted = jnp.dot(metric_ref[...], turned_ref[i], preferred_element_type=jnp.float32)
    out = []
    for b in range(2):
        column = fitted[:, b * BS : (b + 1) * BS]
        pieces = [column[q * QB : (q + 1) * QB] * mask_ref[q, b] for q in range(4)]
        out.append(jnp.concatenate(pieces, axis=0).astype(jnp.bfloat16))
    return out


def fit_kernel(rows_a, rows_b, perm_ref, metric_ref, mask_ref, out_a, out_b, turned_ref):
    turn_rows((rows_a, rows_b), perm_ref, turned_ref, 0, 16)

    def fit(i, carry):
        at = pl.multiple_of(i * 512, 512)
        out_a[pl.ds(at, 512), :], out_b[pl.ds(at, 512), :] = fit_one(metric_ref, turned_ref, mask_ref, i)
        return carry

    lax.fori_loop(0, 8, fit, 0, unroll=4)


def whole(shape, at=None):
    return pl.BlockSpec(shape, lambda g: at or (0,) * len(shape))


def fit_chunk(rows, pair, perm, metric, mask):
    return pl.pallas_call(
        fit_kernel,
        grid=(1,),
        out_shape=[jax.ShapeDtypeStruct((4096, BS), jnp.bfloat16)] * 2,
        in_specs=[
            whole((4096, BS), (0, FIRST.index(pair[0]))),
            whole((4096, BS), (0, FIRST.index(pair[1]))),
            whole((256, 256)),
            whole((512, 512)),
            pl.BlockSpec(memory_space=SMEM),
        ],
        out_specs=[whole((4096, BS))] * 2,
        scratch_shapes=[pltpu.VMEM((8, 512, PAIR), jnp.bfloat16)],
        compiler_params=pltpu.CompilerParams(vmem_limit_bytes=24 << 20),
        cost_estimate=pl.CostEstimate(flops=2 * 4096 * PAIR * 768, bytes_accessed=4 * 4096 * PAIR, transcendentals=0),
        name="fit_chunk",
    )(rows, rows, perm, metric, mask)


def quarter(tile_ref, row, col, which):
    at = pl.multiple_of(row * BS + lax.rem(which, NY) * PART, PART)
    return tile_ref[pl.ds(at, PART), col * BS : (col + 1) * BS]


def put_sent(out_ref, n, low_at, value):
    high = value.astype(jnp.bfloat16)
    out_ref[n] = high
    if low_at is not None:
        out_ref[low_at] = (value - high.astype(jnp.float32)).astype(jnp.bfloat16)


def put_slot(tile_ref, row, col, n, diagonal, slots, off, y, own_ref, out_refs):
    for d in range(NY):
        at = pl.multiple_of(row * BS + lax.rem(y + d, NY) * PART, PART)
        piece = tile_ref[pl.ds(at, PART), col * BS : (col + 1) * BS]
        if d == 0:
            own_ref[n] = piece
            continue
        high = piece.astype(jnp.bfloat16)
        out_refs[d - 1][n] = high
        if diagonal:
            out_refs[d - 1][n + len(slots) - off] = (piece - high.astype(jnp.float32)).astype(jnp.bfloat16)


def put_tiles(found, tiles, flip_ref, slots, off, y, own_ref, out_refs):
    flips = 0
    for r, e in slots:
        if (r, e) not in found:
            continue
        product, s, t, turned = found[r, e]
        n = slots.index((r, e))
        if not turned:
            put_slot(tiles[product], s, t, n, e == 0, slots, off, y, own_ref, out_refs)
            continue
        flip_ref[flips] = tiles[product][s * BS : (s + 1) * BS, t * BS : (t + 1) * BS].T
        put_slot(flip_ref.at[flips], 0, 0, n, False, slots, off, y, own_ref, out_refs)
        flips += 1


EARLY_BLOCKS = (0, 1, 2, 5, 6, 7)


def early_kernel(y_ref, *refs):
    blocks = dict(zip(EARLY_BLOCKS, refs[:6]))
    own_ref, o1, o2, o3, t0, t1, t2, flip_ref = refs[6:]
    tiles = (t0, t1, t2)
    for n, (rows, cols) in enumerate(EARLY_PRODUCTS):
        left = jnp.concatenate([blocks[r][...] for r in rows], axis=1).T
        right = jnp.concatenate([blocks[k][...] for k in cols], axis=1)
        tiles[n][...] = jnp.dot(left, right, preferred_element_type=jnp.float32)
    put_tiles(EARLY_TILES, tiles, flip_ref, EARLY, EARLY_OFF, y_ref[0], own_ref, (o1, o2, o3))


def edge_kernel(below, f0, f1, f6, f7, above, down_ref, up_ref, own_ref):
    low = jnp.dot(
        below[...].T, jnp.concatenate([f0[...], f1[...]], axis=1), preferred_element_type=jnp.float32
    )
    high = jnp.dot(
        above[...].T, jnp.concatenate([f6[...], f7[...]], axis=1), preferred_element_type=jnp.float32
    )
    down_ref[...] = low[:, BS:]
    up_ref[...] = high[:, :BS]
    own_ref[0] = low[:, :BS].T
    own_ref[1] = low[:, BS:].T
    own_ref[2] = high[:, :BS].T
    own_ref[3] = high[:, BS:].T


def edge_tiles(below, f0, f1, f6, f7, above):
    tile = jax.ShapeDtypeStruct((BS, BS), jnp.float32)
    return pl.pallas_call(
        edge_kernel,
        out_shape=[tile, tile, jax.ShapeDtypeStruct((4, BS, BS), jnp.float32)],
        in_specs=[pl.BlockSpec(memory_space=VMEM)] * 6,
        out_specs=[pl.BlockSpec(memory_space=VMEM)] * 3,
        compiler_params=pltpu.CompilerParams(vmem_limit_bytes=24 << 20),
        cost_estimate=pl.CostEstimate(flops=2 * 4096 * 256 * 256, bytes_accessed=6 << 20, transcendentals=0),
        name="edge_tiles",
    )(below, f0, f1, f6, f7, above)


def late_kernel(y_ref, mask_ref, rows_hbm, f1_hbm, f2_hbm, f5_hbm, f6_hbm, perm_ref, metric_ref, from_below, from_above, edges, own_ref, *rest):
    outs, (rows_ref, turned_ref, left_ref, right_ref, tiles_ref, flip_ref, row_sems, sems) = rest[:7], rest[7:]
    feeds = []
    for n in range(4):
        piece = pl.ds(n * 1024, 1024)
        feeds.append(pltpu.make_async_copy(rows_hbm.at[piece], rows_ref.at[piece], row_sems.at[n]))
    fits = [
        pltpu.make_async_copy(f, right_ref.at[n], sems.at[n]) for n, f in enumerate((f1_hbm, f2_hbm, f5_hbm, f6_hbm))
    ]
    for copy in feeds + fits:
        copy.start()
    for n, feed in enumerate(feeds):
        feed.wait()
        turn_rows((rows_ref,), perm_ref, turned_ref, 4 * n, 4)

    def step(i, carry):
        at = pl.ds(pl.multiple_of(i * 512, 512), 512)
        left_ref[at, :BS], left_ref[at, BS:] = fit_one(metric_ref, turned_ref, mask_ref, i)
        return carry

    lax.fori_loop(0, 8, step, 0, unroll=4)
    for copy in fits:
        copy.wait()
    f1, f2, f5, f6 = [right_ref[n] for n in range(4)]
    right = jnp.concatenate([f1, f2, left_ref[...], f5, f6], axis=1)
    tiles_ref[...] = jnp.dot(left_ref[...].T, right, preferred_element_type=jnp.float32)
    at = {(0, -2): (from_below, 0, 0), (7, 2): (from_above, 0, 0)}
    for n, slot in enumerate(STRANGE[2:]):
        at[slot] = (edges.at[n], 0, 0)
    flips = 0
    for slot, (_, s, t, turned) in LATE_TILES.items():
        if turned:
            flip_ref[flips] = tiles_ref[s * BS : (s + 1) * BS, t * BS : (t + 1) * BS].T
            at[slot] = (flip_ref.at[flips], 0, 0)
            flips += 1
        else:
            at[slot] = (tiles_ref, s, t)
    y, odd = y_ref[0], y_ref[1]
    for n in range(LATE_HALF):
        for d in range(NY):
            even_piece, odd_piece = [quarter(*at[LATE_BY[k][n]], y + d) for k in range(2)]
            mine = jnp.where(odd == 0, even_piece, odd_piece)
            theirs = jnp.where(odd == 0, odd_piece, even_piece)
            low_at = n + LATE_DIAGONALS if n >= LATE_HALF - LATE_DIAGONALS else None
            if d == 0:
                own_ref[n] = mine
            else:
                put_sent(outs[d - 1], n, low_at, mine)
            put_sent(outs[3 + d], n, low_at, theirs)


def exchange_shapes(slots, off):
    sent = jax.ShapeDtypeStruct((sent_slots(slots, off), PART, BS), jnp.bfloat16)
    return [jax.ShapeDtypeStruct((len(slots), PART, BS), jnp.float32)] + [sent] * 3


def early_tiles(y, blocks):
    return pl.pallas_call(
        early_kernel,
        out_shape=exchange_shapes(EARLY, EARLY_OFF),
        in_specs=[pl.BlockSpec(memory_space=SMEM)] + [pl.BlockSpec(memory_space=VMEM)] * 6,
        out_specs=[pl.BlockSpec(memory_space=VMEM)] * 4,
        scratch_shapes=[
            pltpu.VMEM((PAIR, 3 * BS), jnp.float32),
            pltpu.VMEM((PAIR, 3 * BS), jnp.float32),
            pltpu.VMEM((PAIR, PAIR), jnp.float32),
            pltpu.VMEM((4, BS, BS), jnp.float32),
        ],
        compiler_params=pltpu.CompilerParams(vmem_limit_bytes=40 << 20),
        cost_estimate=pl.CostEstimate(flops=2 * 4096 * 256 * 1024, bytes_accessed=7 << 20, transcendentals=0),
        name="early_tiles",
    )(y, *blocks)


def late_tiles(y, mask, rows, f1, f2, f5, f6, perm, metric, from_below, from_above, edges):
    return pl.pallas_call(
        late_kernel,
        out_shape=[jax.ShapeDtypeStruct((LATE_HALF, PART, BS), jnp.float32)]
        + [jax.ShapeDtypeStruct((LATE_HALF + LATE_DIAGONALS, PART, BS), jnp.bfloat16)] * 7,
        in_specs=[pl.BlockSpec(memory_space=SMEM)] * 2
        + [pl.BlockSpec(memory_space=pl.ANY)] * 5
        + [pl.BlockSpec(memory_space=VMEM)] * 5,
        out_specs=[pl.BlockSpec(memory_space=VMEM)] * 8,
        scratch_shapes=[
            pltpu.VMEM((4096, PAIR), jnp.bfloat16),
            pltpu.VMEM((8, 512, PAIR), jnp.bfloat16),
            pltpu.VMEM((4096, PAIR), jnp.bfloat16),
            pltpu.VMEM((4, 4096, BS), jnp.bfloat16),
            pltpu.VMEM((PAIR, 6 * BS), jnp.float32),
            pltpu.VMEM((6, BS, BS), jnp.float32),
            pltpu.SemaphoreType.DMA((4,)),
            pltpu.SemaphoreType.DMA((4,)),
        ],
        compiler_params=pltpu.CompilerParams(vmem_limit_bytes=52 << 20),
        cost_estimate=pl.CostEstimate(flops=2 * 4096 * 256 * 1536, bytes_accessed=8 << 20, transcendentals=0),
        name="late_tiles",
    )(y, mask, rows, f1, f2, f5, f6, perm, metric, from_below, from_above, edges)


def over_domains(sent):
    return [lax.ppermute(s, "aux", [(a, (a + d) % NY) for a in range(NY)]) for d, s in enumerate(sent, 1)]


def gathered(own_ref, got_refs, n, low_at):
    value = own_ref[n]
    for got in got_refs:
        value = value + got[n].astype(jnp.float32)
        if low_at is not None:
            value = value + got[low_at].astype(jnp.float32)
    return value


def early_sum_kernel(odd_ref, own_ref, g1, g2, g3, mine_ref, theirs_ref):
    odd = odd_ref[0]
    for n in range(EARLY_HALF):
        pair = []
        for k in range(2):
            r, e = EARLY_BY[k][n]
            m = EARLY.index((r, e))
            pair.append(gathered(own_ref, (g1, g2, g3), m, m + len(EARLY) - EARLY_OFF if e == 0 else None))
        low_at = n + EARLY_DIAGONALS if n >= EARLY_HALF - EARLY_DIAGONALS else None
        mine_ref[n] = jnp.where(odd == 0, pair[0], pair[1])
        put_sent(theirs_ref, n, low_at, jnp.where(odd == 0, pair[1], pair[0]))


def early_sum(odd, own, got):
    return pl.pallas_call(
        early_sum_kernel,
        out_shape=[
            jax.ShapeDtypeStruct((EARLY_HALF, PART, BS), jnp.float32),
            jax.ShapeDtypeStruct((EARLY_HALF + EARLY_DIAGONALS, PART, BS), jnp.bfloat16),
        ],
        in_specs=[pl.BlockSpec(memory_space=SMEM)] + [pl.BlockSpec(memory_space=VMEM)] * 4,
        out_specs=[pl.BlockSpec(memory_space=VMEM)] * 2,
        compiler_params=pltpu.CompilerParams(vmem_limit_bytes=16 << 20),
        name="early_sum",
    )(odd, own, *got)


def settle_kernel(z_ref, early_ref, early_got, late_ref, *rest):
    late_got, (own_ref, o1, o2, o3, band_ref) = rest[:7], rest[7:]
    odd, half = lax.rem(z_ref[0], 2), lax.div(z_ref[0], 2)

    def place(by, n, value):
        (r0, e0), (r1, e1) = by[0][n], by[1][n]
        band_ref[jnp.where(odd == 0, r0 // 2, r1 // 2), jnp.where(odd == 0, e0 + 2, e1 + 2)] = value

    for n in range(EARLY_HALF):
        low_at = n + EARLY_DIAGONALS if n >= EARLY_HALF - EARLY_DIAGONALS else None
        place(EARLY_BY, n, gathered(early_ref, (early_got,), n, low_at))
    for n in range(LATE_HALF):
        low_at = n + LATE_DIAGONALS if n >= LATE_HALF - LATE_DIAGONALS else None
        place(LATE_BY, n, gathered(late_ref, late_got, n, low_at))
    for j, out in enumerate((own_ref, o1, o2, o3)):
        k = lax.rem(half + j, 4)
        for slot in range(BAND):
            out[:, slot * BS : (slot + 1) * BS] = band_ref[k, slot]


def settle(z, early, early_got, late, late_got):
    return pl.pallas_call(
        settle_kernel,
        out_shape=[jax.ShapeDtypeStruct((PART, BAND * BS), jnp.float32)] * 4,
        in_specs=[pl.BlockSpec(memory_space=SMEM)] + [pl.BlockSpec(memory_space=VMEM)] * 10,
        out_specs=[pl.BlockSpec(memory_space=VMEM)] * 4,
        scratch_shapes=[pltpu.VMEM((4, BAND, PART, BS), jnp.float32)],
        compiler_params=pltpu.CompilerParams(vmem_limit_bytes=16 << 20),
        name="settle",
    )(z, early, early_got, late, *late_got)


def local(integrals, metric, pair_list, aux_mask):
    blk = lax.axis_index("blk")
    z, c = blk // NC, blk % NC
    y = jnp.stack([lax.axis_index("aux"), z % 2]).astype(jnp.int32)
    at_z = jnp.full((1,), z, jnp.int32)
    grid = [(k // NC, k % NC) for k in range(NZ * NC)]
    up = [(zz * NC + cc, zz * NC + cc + 1) for zz, cc in grid if cc < NC - 1]
    down = [(b, a) for a, b in up]

    row = lax.broadcasted_iota(jnp.int32, (256, 256), 0)
    col = lax.broadcasted_iota(jnp.int32, (256, 256), 1)
    perm = ((row // 32 == col % 8) & (row % 32 == col // 8)).astype(jnp.bfloat16)
    own_mask = lax.dynamic_slice(aux_mask, (0, c * 8), (4, 8)).astype(jnp.float32)
    mask_of = lambda *blocks: jnp.stack([own_mask[:, b] for b in blocks], axis=1)

    e = jnp.arange(BAND, dtype=jnp.int32) - 2
    home = c * NC + z
    low, high = home + jnp.minimum(e, 0), home + jnp.maximum(e, 0)
    hits = (pair_list[:, 0][:, None] == low[None]) & (pair_list[:, 1][:, None] == high[None])
    scale = jnp.repeat(jnp.sum(hits.astype(jnp.float32), axis=0), BS)

    whole_grid = [(a, zz, cc) for a in range(NY) for zz, cc in grid]

    def move(array, d, flip):
        pairs = [
            (a * NZ * NC + zz * NC + cc, (a + d) % NY * NZ * NC + (zz ^ flip) * NC + cc) for a, zz, cc in whole_grid
        ]
        return lax.ppermute(array, AXES, pairs)

    def spread(blocks, source):
        got = lax.all_to_all(cut_chunk(source, blocks), "blk", split_axis=0, concat_axis=0, tiled=True)
        return got.reshape(4096, BS * len(blocks))

    rows = spread(FIRST, integrals)
    last = spread(LAST, integrals)
    f0, f7 = fit_chunk(rows, (0, 7), perm, metric, mask_of(0, 7))
    above = lax.ppermute(f0, "blk", down)
    below = lax.ppermute(f7, "blk", up)
    f1, f2 = fit_chunk(rows, (1, 2), perm, metric, mask_of(1, 2))
    f5, f6 = fit_chunk(rows, (5, 6), perm, metric, mask_of(5, 6))

    early, *sent = early_tiles(y, (f0, f1, f2, f5, f6, f7))
    early, early_sent = early_sum(jnp.full((1,), z % 2, jnp.int32), early, over_domains(sent))
    to_below, to_above, edges = edge_tiles(below, f0, f1, f6, f7, above)
    from_above = lax.ppermute(to_below, "blk", down)
    from_below = lax.ppermute(to_above, "blk", up)
    early_got = move(early_sent, 0, 1)
    early_got, from_above, from_below, last = lax.optimization_barrier((early_got, from_above, from_below, last))

    late, *sent = late_tiles(y, mask_of(3, 4), last, f1, f2, f5, f6, perm, metric, from_below, from_above, edges)
    late_got = [move(s, d, 0) for d, s in enumerate(sent[:3], 1)] + [move(s, d, 1) for d, s in enumerate(sent[3:])]
    total, *sent = settle(at_z, early, early_got, late, late_got)
    for j, s in enumerate(sent, 1):
        total = total + lax.ppermute(s, "blk", [(zz * NC + cc, (zz + 2 * j) % NZ * NC + cc) for zz, cc in grid])
    total = (total * scale[None, :])[None]
    return lax.ppermute(total, "blk", [(zz * NC + cc, cc * NC + zz) for zz, cc in grid])


def solution(mesh):
    return jax.shard_map(
        local,
        mesh=mesh,
        in_specs=(P(("aux", "blk"), None, None), P("aux", None), P(), P("aux", None)),
        out_specs=P("blk", "aux", None),
        check_vma=False,
    )
```

```python
import jax
import jax.numpy as jnp
from jax import lax
from jax.experimental import pallas as pl
from jax.experimental.pallas import tpu as pltpu
from jax.sharding import PartitionSpec as P

BS = 128
QB = 128
NZ = 8
NC = 8
NY = 4
PAIR = 2 * BS
BAND = 5
PART = BS // NY
PARTS = 2
FIRST = (0, 7, 1, 2, 5, 6)
LAST = (3, 4)
VMEM = pltpu.MemorySpace.VMEM
SMEM = pltpu.MemorySpace.SMEM

EARLY_PRODUCTS = (((0, 1), (0, 1, 2)), ((6, 7), (5, 6, 7)), ((2, 5), (2, 5)))
LATE_PRODUCT = ((3, 4), (1, 2, 3, 4, 5, 6))


def tiles_of(products):
    found = {}
    for n, (rows, cols) in enumerate(products):
        for s, r in enumerate(rows):
            for t, k in enumerate(cols):
                if abs(k - r) <= 2:
                    found[r, k - r] = (n, s, t, False)
    for n, (rows, cols) in enumerate(products):
        for s, r in enumerate(rows):
            for t, k in enumerate(cols):
                if abs(k - r) <= 2 and 0 <= k < NC and (k, r - k) not in found:
                    found[k, r - k] = (n, s, t, True)
    return found


EARLY_TILES = tiles_of(EARLY_PRODUCTS)
LATE_TILES = tiles_of((LATE_PRODUCT,))
STRANGE = ((0, -2), (7, 2), (0, -1), (1, -2), (6, 2), (7, 1))


def ordered(slots):
    off = [k for k in slots if k[1] != 0]
    return off + [k for k in slots if k[1] == 0], len(off)


def of_parity(slots, odd):
    return ordered([k for k in slots if k[0] % 2 == odd])[0]


EARLY, EARLY_OFF = ordered(EARLY_TILES)
EARLY_BY = [of_parity(EARLY, odd) for odd in range(2)]
LATE_ALL = STRANGE + tuple(LATE_TILES)
LATE_BY = [of_parity(LATE_ALL, odd) for odd in range(2)]
EARLY_HALF = len(EARLY_BY[0])
LATE_HALF = len(LATE_BY[0])
LATE_DIAGONALS = 1
EARLY_DIAGONALS = 3
AXES = ("aux", "blk")


def sent_slots(slots, off):
    return 2 * len(slots) - off


def runs(blocks):
    found = []
    for n, b in enumerate(blocks):
        if found and found[-1][0] + found[-1][2] == b * BS:
            found[-1][2] += BS
        else:
            found.append([b * BS, n * BS, BS])
    return found


def cut_kernel(source, out_ref, held, sems, *, blocks):
    size = NZ * NC // PARTS

    def gather(part):
        def one(n, carry):
            k = part * size + n
            z, c = k // NC, k % NC
            for start, at, width in runs(blocks):
                begin = pl.multiple_of(c * 1024 + start, BS)
                pltpu.make_async_copy(
                    source.at[:, z, :, pl.ds(begin, width)], held.at[k, :, :, pl.ds(at, width)], sems.at[part]
                ).start()
            return carry

        lax.fori_loop(0, size, one, 0)

    for part in range(PARTS):
        gather(part)
    writes = []
    for part in range(PARTS):
        here = held.at[pl.ds(part * size, size)]
        pltpu.make_async_copy(here, here, sems.at[part]).wait()
        write = pltpu.make_async_copy(here, out_ref.at[pl.ds(part * size, size)], sems.at[PARTS + part])
        write.start()
        writes.append(write)
    for write in writes:
        write.wait()


def cut_chunk(integrals, blocks):
    shape = (NZ * NC, 8, 8, BS * len(blocks))
    return pl.pallas_call(
        lambda *refs: cut_kernel(*refs, blocks=blocks),
        out_shape=jax.ShapeDtypeStruct(shape, jnp.bfloat16),
        in_specs=[pl.BlockSpec(memory_space=pl.ANY)],
        out_specs=pl.BlockSpec(memory_space=pl.ANY),
        scratch_shapes=[pltpu.VMEM(shape, jnp.bfloat16), pltpu.SemaphoreType.DMA((2 * PARTS,))],
        compiler_params=pltpu.CompilerParams(vmem_limit_bytes=60 << 20),
        cost_estimate=pl.CostEstimate(flops=0, bytes_accessed=2 * 8192 * shape[3], transcendentals=0),
        name="cut_chunk",
    )(integrals.reshape(8, NZ, 8, NC * 1024))


def turn_rows(rows_refs, perm_ref, turned_ref, first, count):
    def turn(g, carry):
        start = pl.multiple_of(g * 256, 256)
        rows = jnp.concatenate([rows_ref[pl.ds(start, 256), :] for rows_ref in rows_refs], axis=1)
        turned = jnp.dot(perm_ref[...], rows, preferred_element_type=jnp.float32)
        turned = turned.astype(jnp.bfloat16)
        at = pl.multiple_of(g * 32, 32)
        for i in range(8):
            turned_ref[i, pl.ds(at, 32), :] = turned[i * 32 : (i + 1) * 32]
        return carry

    lax.fori_loop(first, first + count, turn, 0, unroll=8)


def fit_one(metric_ref, turned_ref, mask_ref, i):
    fitted = jnp.dot(metric_ref[...], turned_ref[i], preferred_element_type=jnp.float32)
    out = []
    for b in range(2):
        column = fitted[:, b * BS : (b + 1) * BS]
        pieces = [column[q * QB : (q + 1) * QB] * mask_ref[q, b] for q in range(4)]
        out.append(jnp.concatenate(pieces, axis=0).astype(jnp.bfloat16))
    return out


def fit_kernel(rows_a, rows_b, perm_ref, metric_ref, mask_ref, out_a, out_b, turned_ref):
    turn_rows((rows_a, rows_b), perm_ref, turned_ref, 0, 16)

    def fit(i, carry):
        at = pl.multiple_of(i * 512, 512)
        out_a[pl.ds(at, 512), :], out_b[pl.ds(at, 512), :] = fit_one(metric_ref, turned_ref, mask_ref, i)
        return carry

    lax.fori_loop(0, 8, fit, 0, unroll=2)


def whole(shape, at=None):
    return pl.BlockSpec(shape, lambda g: at or (0,) * len(shape))


def fit_chunk(rows, pair, perm, metric, mask):
    return pl.pallas_call(
        fit_kernel,
        grid=(1,),
        out_shape=[jax.ShapeDtypeStruct((4096, BS), jnp.bfloat16)] * 2,
        in_specs=[
            whole((4096, BS), (0, FIRST.index(pair[0]))),
            whole((4096, BS), (0, FIRST.index(pair[1]))),
            whole((256, 256)),
            whole((512, 512)),
            pl.BlockSpec(memory_space=SMEM),
        ],
        out_specs=[whole((4096, BS))] * 2,
        scratch_shapes=[pltpu.VMEM((8, 512, PAIR), jnp.bfloat16)],
        compiler_params=pltpu.CompilerParams(vmem_limit_bytes=24 << 20),
        cost_estimate=pl.CostEstimate(flops=2 * 4096 * PAIR * 768, bytes_accessed=4 * 4096 * PAIR, transcendentals=0),
        name="fit_chunk",
    )(rows, rows, perm, metric, mask)


def quarter(tile_ref, row, col, which):
    at = pl.multiple_of(row * BS + lax.rem(which, NY) * PART, PART)
    return tile_ref[pl.ds(at, PART), col * BS : (col + 1) * BS]


def put_sent(out_ref, n, low_at, value):
    high = value.astype(jnp.bfloat16)
    out_ref[n] = high
    if low_at is not None:
        out_ref[low_at] = (value - high.astype(jnp.float32)).astype(jnp.bfloat16)


def put_slot(tile_ref, row, col, n, diagonal, slots, off, y, own_ref, out_refs):
    for d in range(NY):
        at = pl.multiple_of(row * BS + lax.rem(y + d, NY) * PART, PART)
        piece = tile_ref[pl.ds(at, PART), col * BS : (col + 1) * BS]
        if d == 0:
            own_ref[n] = piece
            continue
        high = piece.astype(jnp.bfloat16)
        out_refs[d - 1][n] = high
        if diagonal:
            out_refs[d - 1][n + len(slots) - off] = (piece - high.astype(jnp.float32)).astype(jnp.bfloat16)


def put_tiles(found, tiles, flip_ref, slots, off, y, own_ref, out_refs):
    flips = 0
    for r, e in slots:
        if (r, e) not in found:
            continue
        product, s, t, turned = found[r, e]
        n = slots.index((r, e))
        if not turned:
            put_slot(tiles[product], s, t, n, e == 0, slots, off, y, own_ref, out_refs)
            continue
        flip_ref[flips] = tiles[product][s * BS : (s + 1) * BS, t * BS : (t + 1) * BS].T
        put_slot(flip_ref.at[flips], 0, 0, n, False, slots, off, y, own_ref, out_refs)
        flips += 1


EARLY_BLOCKS = (0, 1, 2, 5, 6, 7)


def early_kernel(y_ref, *refs):
    blocks = dict(zip(EARLY_BLOCKS, refs[:6]))
    own_ref, o1, o2, o3, t0, t1, t2, flip_ref = refs[6:]
    tiles = (t0, t1, t2)
    for n, (rows, cols) in enumerate(EARLY_PRODUCTS):
        left = jnp.concatenate([blocks[r][...] for r in rows], axis=1).T
        right = jnp.concatenate([blocks[k][...] for k in cols], axis=1)
        tiles[n][...] = jnp.dot(left, right, preferred_element_type=jnp.float32)
    put_tiles(EARLY_TILES, tiles, flip_ref, EARLY, EARLY_OFF, y_ref[0], own_ref, (o1, o2, o3))


def edge_kernel(below, f0, f1, f6, f7, above, down_ref, up_ref, own_ref):
    low = jnp.dot(
        below[...].T, jnp.concatenate([f0[...], f1[...]], axis=1), preferred_element_type=jnp.float32
    )
    high = jnp.dot(
        above[...].T, jnp.concatenate([f6[...], f7[...]], axis=1), preferred_element_type=jnp.float32
    )
    down_ref[...] = low[:, BS:]
    up_ref[...] = high[:, :BS]
    own_ref[0] = low[:, :BS].T
    own_ref[1] = low[:, BS:].T
    own_ref[2] = high[:, :BS].T
    own_ref[3] = high[:, BS:].T


def edge_tiles(below, f0, f1, f6, f7, above):
    tile = jax.ShapeDtypeStruct((BS, BS), jnp.float32)
    return pl.pallas_call(
        edge_kernel,
        out_shape=[tile, tile, jax.ShapeDtypeStruct((4, BS, BS), jnp.float32)],
        in_specs=[pl.BlockSpec(memory_space=VMEM)] * 6,
        out_specs=[pl.BlockSpec(memory_space=VMEM)] * 3,
        compiler_params=pltpu.CompilerParams(vmem_limit_bytes=24 << 20),
        cost_estimate=pl.CostEstimate(flops=2 * 4096 * 256 * 256, bytes_accessed=6 << 20, transcendentals=0),
        name="edge_tiles",
    )(below, f0, f1, f6, f7, above)


def late_kernel(y_ref, mask_ref, rows_hbm, f1_hbm, f2_hbm, f5_hbm, f6_hbm, perm_ref, metric_ref, from_below, from_above, edges, own_ref, *rest):
    outs, (rows_ref, turned_ref, left_ref, right_ref, tiles_ref, flip_ref, row_sems, sems) = rest[:7], rest[7:]
    feeds = []
    for n in range(2):
        piece = pl.ds(n * 2048, 2048)
        feeds.append(pltpu.make_async_copy(rows_hbm.at[piece], rows_ref.at[piece], row_sems.at[n]))
    fits = [
        pltpu.make_async_copy(f, right_ref.at[n], sems.at[n]) for n, f in enumerate((f1_hbm, f2_hbm, f5_hbm, f6_hbm))
    ]
    for copy in feeds + fits:
        copy.start()
    for n, feed in enumerate(feeds):
        feed.wait()
        turn_rows((rows_ref,), perm_ref, turned_ref, 8 * n, 8)

    def step(i, carry):
        at = pl.ds(pl.multiple_of(i * 512, 512), 512)
        left_ref[at, :BS], left_ref[at, BS:] = fit_one(metric_ref, turned_ref, mask_ref, i)
        return carry

    lax.fori_loop(0, 8, step, 0, unroll=4)
    for copy in fits:
        copy.wait()
    f1, f2, f5, f6 = [right_ref[n] for n in range(4)]
    right = jnp.concatenate([f1, f2, left_ref[...], f5, f6], axis=1)
    tiles_ref[...] = jnp.dot(left_ref[...].T, right, preferred_element_type=jnp.float32)
    at = {(0, -2): (from_below, 0, 0), (7, 2): (from_above, 0, 0)}
    for n, slot in enumerate(STRANGE[2:]):
        at[slot] = (edges.at[n], 0, 0)
    flips = 0
    for slot, (_, s, t, turned) in LATE_TILES.items():
        if turned:
            flip_ref[flips] = tiles_ref[s * BS : (s + 1) * BS, t * BS : (t + 1) * BS].T
            at[slot] = (flip_ref.at[flips], 0, 0)
            flips += 1
        else:
            at[slot] = (tiles_ref, s, t)
    y, odd = y_ref[0], y_ref[1]
    for n in range(LATE_HALF):
        for d in range(NY):
            even_piece, odd_piece = [quarter(*at[LATE_BY[k][n]], y + d) for k in range(2)]
            mine = jnp.where(odd == 0, even_piece, odd_piece)
            theirs = jnp.where(odd == 0, odd_piece, even_piece)
            low_at = n + LATE_DIAGONALS if n >= LATE_HALF - LATE_DIAGONALS else None
            if d == 0:
                own_ref[n] = mine
            else:
                put_sent(outs[d - 1], n, low_at, mine)
            put_sent(outs[3 + d], n, low_at, theirs)


def exchange_shapes(slots, off):
    sent = jax.ShapeDtypeStruct((sent_slots(slots, off), PART, BS), jnp.bfloat16)
    return [jax.ShapeDtypeStruct((len(slots), PART, BS), jnp.float32)] + [sent] * 3


def early_tiles(y, blocks):
    return pl.pallas_call(
        early_kernel,
        out_shape=exchange_shapes(EARLY, EARLY_OFF),
        in_specs=[pl.BlockSpec(memory_space=SMEM)] + [pl.BlockSpec(memory_space=VMEM)] * 6,
        out_specs=[pl.BlockSpec(memory_space=VMEM)] * 4,
        scratch_shapes=[
            pltpu.VMEM((PAIR, 3 * BS), jnp.float32),
            pltpu.VMEM((PAIR, 3 * BS), jnp.float32),
            pltpu.VMEM((PAIR, PAIR), jnp.float32),
            pltpu.VMEM((4, BS, BS), jnp.float32),
        ],
        compiler_params=pltpu.CompilerParams(vmem_limit_bytes=40 << 20),
        cost_estimate=pl.CostEstimate(flops=2 * 4096 * 256 * 1024, bytes_accessed=7 << 20, transcendentals=0),
        name="early_tiles",
    )(y, *blocks)


def late_tiles(y, mask, rows, f1, f2, f5, f6, perm, metric, from_below, from_above, edges):
    return pl.pallas_call(
        late_kernel,
        out_shape=[jax.ShapeDtypeStruct((LATE_HALF, PART, BS), jnp.float32)]
        + [jax.ShapeDtypeStruct((LATE_HALF + LATE_DIAGONALS, PART, BS), jnp.bfloat16)] * 7,
        in_specs=[pl.BlockSpec(memory_space=SMEM)] * 2
        + [pl.BlockSpec(memory_space=pl.ANY)] * 5
        + [pl.BlockSpec(memory_space=VMEM)] * 5,
        out_specs=[pl.BlockSpec(memory_space=VMEM)] * 8,
        scratch_shapes=[
            pltpu.VMEM((4096, PAIR), jnp.bfloat16),
            pltpu.VMEM((8, 512, PAIR), jnp.bfloat16),
            pltpu.VMEM((4096, PAIR), jnp.bfloat16),
            pltpu.VMEM((4, 4096, BS), jnp.bfloat16),
            pltpu.VMEM((PAIR, 6 * BS), jnp.float32),
            pltpu.VMEM((6, BS, BS), jnp.float32),
            pltpu.SemaphoreType.DMA((4,)),
            pltpu.SemaphoreType.DMA((4,)),
        ],
        compiler_params=pltpu.CompilerParams(vmem_limit_bytes=52 << 20),
        cost_estimate=pl.CostEstimate(flops=2 * 4096 * 256 * 1536, bytes_accessed=8 << 20, transcendentals=0),
        name="late_tiles",
    )(y, mask, rows, f1, f2, f5, f6, perm, metric, from_below, from_above, edges)


def over_domains(sent):
    return [lax.ppermute(s, "aux", [(a, (a + d) % NY) for a in range(NY)]) for d, s in enumerate(sent, 1)]


def gathered(own_ref, got_refs, n, low_at):
    value = own_ref[n]
    for got in got_refs:
        value = value + got[n].astype(jnp.float32)
        if low_at is not None:
            value = value + got[low_at].astype(jnp.float32)
    return value


def early_sum_kernel(odd_ref, own_ref, g1, g2, g3, mine_ref, theirs_ref):
    odd = odd_ref[0]
    for n in range(EARLY_HALF):
        pair = []
        for k in range(2):
            r, e = EARLY_BY[k][n]
            m = EARLY.index((r, e))
            pair.append(gathered(own_ref, (g1, g2, g3), m, m + len(EARLY) - EARLY_OFF if e == 0 else None))
        low_at = n + EARLY_DIAGONALS if n >= EARLY_HALF - EARLY_DIAGONALS else None
        mine_ref[n] = jnp.where(odd == 0, pair[0], pair[1])
        put_sent(theirs_ref, n, low_at, jnp.where(odd == 0, pair[1], pair[0]))


def early_sum(odd, own, got):
    return pl.pallas_call(
        early_sum_kernel,
        out_shape=[
            jax.ShapeDtypeStruct((EARLY_HALF, PART, BS), jnp.float32),
            jax.ShapeDtypeStruct((EARLY_HALF + EARLY_DIAGONALS, PART, BS), jnp.bfloat16),
        ],
        in_specs=[pl.BlockSpec(memory_space=SMEM)] + [pl.BlockSpec(memory_space=VMEM)] * 4,
        out_specs=[pl.BlockSpec(memory_space=VMEM)] * 2,
        compiler_params=pltpu.CompilerParams(vmem_limit_bytes=16 << 20),
        name="early_sum",
    )(odd, own, *got)


def settle_kernel(z_ref, early_ref, early_got, late_ref, *rest):
    late_got, (own_ref, o1, o2, o3, band_ref) = rest[:7], rest[7:]
    odd, half = lax.rem(z_ref[0], 2), lax.div(z_ref[0], 2)

    def place(by, n, value):
        (r0, e0), (r1, e1) = by[0][n], by[1][n]
        band_ref[jnp.where(odd == 0, r0 // 2, r1 // 2), jnp.where(odd == 0, e0 + 2, e1 + 2)] = value

    for n in range(EARLY_HALF):
        low_at = n + EARLY_DIAGONALS if n >= EARLY_HALF - EARLY_DIAGONALS else None
        place(EARLY_BY, n, gathered(early_ref, (early_got,), n, low_at))
    for n in range(LATE_HALF):
        low_at = n + LATE_DIAGONALS if n >= LATE_HALF - LATE_DIAGONALS else None
        place(LATE_BY, n, gathered(late_ref, late_got, n, low_at))
    for j, out in enumerate((own_ref, o1, o2, o3)):
        k = lax.rem(half + j, 4)
        for slot in range(BAND):
            out[:, slot * BS : (slot + 1) * BS] = band_ref[k, slot]


def settle(z, early, early_got, late, late_got):
    return pl.pallas_call(
        settle_kernel,
        out_shape=[jax.ShapeDtypeStruct((PART, BAND * BS), jnp.float32)] * 4,
        in_specs=[pl.BlockSpec(memory_space=SMEM)] + [pl.BlockSpec(memory_space=VMEM)] * 10,
        out_specs=[pl.BlockSpec(memory_space=VMEM)] * 4,
        scratch_shapes=[pltpu.VMEM((4, BAND, PART, BS), jnp.float32)],
        compiler_params=pltpu.CompilerParams(vmem_limit_bytes=16 << 20),
        name="settle",
    )(z, early, early_got, late, *late_got)


def local(integrals, metric, pair_list, aux_mask):
    blk = lax.axis_index("blk")
    z, c = blk // NC, blk % NC
    y = jnp.stack([lax.axis_index("aux"), z % 2]).astype(jnp.int32)
    at_z = jnp.full((1,), z, jnp.int32)
    grid = [(k // NC, k % NC) for k in range(NZ * NC)]
    up = [(zz * NC + cc, zz * NC + cc + 1) for zz, cc in grid if cc < NC - 1]
    down = [(b, a) for a, b in up]

    row = lax.broadcasted_iota(jnp.int32, (256, 256), 0)
    col = lax.broadcasted_iota(jnp.int32, (256, 256), 1)
    perm = ((row // 32 == col % 8) & (row % 32 == col // 8)).astype(jnp.bfloat16)
    own_mask = lax.dynamic_slice(aux_mask, (0, c * 8), (4, 8)).astype(jnp.float32)
    mask_of = lambda *blocks: jnp.stack([own_mask[:, b] for b in blocks], axis=1)

    e = jnp.arange(BAND, dtype=jnp.int32) - 2
    home = c * NC + z
    low, high = home + jnp.minimum(e, 0), home + jnp.maximum(e, 0)
    hits = (pair_list[:, 0][:, None] == low[None]) & (pair_list[:, 1][:, None] == high[None])
    scale = jnp.repeat(jnp.sum(hits.astype(jnp.float32), axis=0), BS)

    whole_grid = [(a, zz, cc) for a in range(NY) for zz, cc in grid]

    def move(array, d, flip):
        pairs = [
            (a * NZ * NC + zz * NC + cc, (a + d) % NY * NZ * NC + (zz ^ flip) * NC + cc) for a, zz, cc in whole_grid
        ]
        return lax.ppermute(array, AXES, pairs)

    def spread(blocks, source):
        got = lax.all_to_all(cut_chunk(source, blocks), "blk", split_axis=0, concat_axis=0, tiled=True)
        return got.reshape(4096, BS * len(blocks))

    rows = spread(FIRST, integrals)
    last = spread(LAST, integrals)
    f0, f7 = fit_chunk(rows, (0, 7), perm, metric, mask_of(0, 7))
    above = lax.ppermute(f0, "blk", down)
    below = lax.ppermute(f7, "blk", up)
    f1, f2 = fit_chunk(rows, (1, 2), perm, metric, mask_of(1, 2))
    f5, f6 = fit_chunk(rows, (5, 6), perm, metric, mask_of(5, 6))

    early, *sent = early_tiles(y, (f0, f1, f2, f5, f6, f7))
    early, early_sent = early_sum(jnp.full((1,), z % 2, jnp.int32), early, over_domains(sent))
    to_below, to_above, edges = edge_tiles(below, f0, f1, f6, f7, above)
    from_above = lax.ppermute(to_below, "blk", down)
    from_below = lax.ppermute(to_above, "blk", up)
    early_got = move(early_sent, 0, 1)
    early_got, from_above, from_below, last = lax.optimization_barrier((early_got, from_above, from_below, last))

    late, *sent = late_tiles(y, mask_of(3, 4), last, f1, f2, f5, f6, perm, metric, from_below, from_above, edges)
    late_got = [move(s, d, 0) for d, s in enumerate(sent[:3], 1)] + [move(s, d, 1) for d, s in enumerate(sent[3:])]
    total, *sent = settle(at_z, early, early_got, late, late_got)
    for j, s in enumerate(sent, 1):
        total = total + lax.ppermute(s, "blk", [(zz * NC + cc, (zz + 2 * j) % NZ * NC + cc) for zz, cc in grid])
    total = (total * scale[None, :])[None]
    return lax.ppermute(total, "blk", [(zz * NC + cc, cc * NC + zz) for zz, cc in grid])


def solution(mesh):
    return jax.shard_map(
        local,
        mesh=mesh,
        in_specs=(P(("aux", "blk"), None, None), P("aux", None), P(), P("aux", None)),
        out_specs=P("blk", "aux", None),
        check_vma=False,
    )
```
